512 devices in a mesh: psg: 128 (over z, y, core), row: 4 (over x).
Axes of the slice: x: 4, y: 8, z: 8, core: 2. Of those that a mesh axis runs over, the one named last changes fastest.
Arguments:
- query: bfloat16 [384, 4096], P('row'), may hold values from -3 to 3
- out_grad: bfloat16 [384, 4096], P('row'), may hold values from -5120 to 5120
- keys: bfloat16 [16384, 4096], P('psg', 'row'), may hold values from -1.5 to 1.5
- values: bfloat16 [16384, 4096], P('psg', 'row'), may hold values from -1.5 to 1.5
Outputs:
- query_grad: bfloat16 [384, 4096], P('row')
- key_grad: bfloat16 [16384, 4096], P('psg', 'row')
- value_grad: bfloat16 [16384, 4096], P('psg', 'row')
The draws below stay inside these ranges and needn't reach their ends.
All inputs are finite; a program needn't handle non-finite values.
Results may differ from the reference program's by a relative error of at most 0.0073.
Values may be sent and summed in bfloat16 or wider, within the bound.
No kernel may reach another device: no remote copies, remote signals or barrier semaphores. Data moves between devices by JAX's collectives and lax.ppermute only.
A program may use at most 64 MiB of HBM per device.

```python
import jax
import jax.numpy as jnp
from jax import lax

H = 64
DH = 64
HD = 4096
ROWS = 384
MEM = 16384


def draw_query(key, part):
    key = jax.random.fold_in(key, 1)
    result = jax.random.truncated_normal(key, -3.0, 3.0, (ROWS, H * DH), jnp.float32)
    return result.astype(jnp.bfloat16)


def draw_keys(key, part):
    key = jax.random.fold_in(key, 3)
    result = 0.125 * jax.random.truncated_normal(key, -8.0, 8.0, (MEM, H * DH), jnp.float32)
    return result.astype(jnp.bfloat16)


def block_scale(rng, dims, pieces, least, largest):
    gain = 1.0
    for axis_at, shards_of in pieces:
        draws = jax.random.uniform(jax.random.fold_in(jax.random.fold_in(rng, 6), axis_at), (shards_of,), jnp.float32, least / len(pieces), largest / len(pieces))
        gain = gain * jnp.repeat(jnp.exp(draws), dims[axis_at] // shards_of).reshape((-1,) + (1,) * (len(dims) - 1 - axis_at))
    return gain


def centred(stream_key, dims, width, reach, pieces=(), kind=jnp.bfloat16):
    values = width * jax.random.normal(stream_key, dims, jnp.float32)
    if pieces:
        values = values * block_scale(stream_key, dims, pieces, -0.22, 0.18)
    return jnp.clip(values, -reach, reach).astype(kind)


def setup_inputs(seed: int = 0) -> dict:
    arg_keys = jax.random.split(jax.random.key(seed), 5)
    return {
        "query": draw_query(jax.random.fold_in(arg_keys[4], 71), 0),
        "out_grad": centred(arg_keys[1], (ROWS, HD), (MEM * 0.05), 5120.0, ((0, 4),)),
        "keys": draw_keys(jax.random.fold_in(arg_keys[4], 71), 0),
        "values": centred(arg_keys[3], (MEM, HD), 0.1, 1.5, ((0, 128), (1, 4))),
    }


def head_terms(parts):
    query_h, grad_h, key_h, value_h = parts
    scores = jnp.dot(query_h, key_h.T, preferred_element_type=jnp.float32)
    peak = jnp.max(scores, axis=1, keepdims=True)
    expo = jnp.exp(scores - peak)
    total = jnp.sum(expo, axis=1, keepdims=True)
    prob = expo / total
    grad_prob = jnp.dot(grad_h, value_h.T, preferred_element_type=jnp.float32)
    offset = jnp.sum(prob * grad_prob, axis=1, keepdims=True)
    grad_score = prob * (grad_prob - offset)
    probability_narrow = prob.astype(jnp.bfloat16)
    score_narrow = grad_score.astype(jnp.bfloat16)
    value_part = jnp.dot(probability_narrow.T, grad_h, preferred_element_type=jnp.float32).astype(jnp.bfloat16)
    key_part = jnp.dot(score_narrow.T, query_h, preferred_element_type=jnp.float32).astype(jnp.bfloat16)
    query_part = jnp.dot(score_narrow, key_h, preferred_element_type=jnp.float32).astype(jnp.bfloat16)
    return query_part, key_part, value_part


def split_heads(array):
    return jnp.transpose(array.reshape(array.shape[0], H, DH), (1, 0, 2))


def join_heads(array):
    return jnp.transpose(array, (1, 0, 2)).reshape(array.shape[1], H * DH)


def reference(query, out_grad, keys, values):
    parts = (split_heads(query), split_heads(out_grad), split_heads(keys), split_heads(values))
    query_part, key_part, value_part = lax.map(head_terms, parts)
    return join_heads(query_part), join_heads(key_part), join_heads(value_part)
```

```python
import jax
import jax.numpy as jnp
from jax import lax
from jax.experimental import pallas as pl
from jax.experimental.pallas import tpu as pltpu
from jax.sharding import Mesh
from jax.sharding import PartitionSpec as P

F32 = jnp.float32
BF16 = jnp.bfloat16
NZ, NY, NC, NX = 8, 8, 2, 4
HEADS = 16
BLOCK = 128
ROWS = 384
MINE = ROWS // NX
MEMS = HEADS * BLOCK
STEP = 256
NT = (((1,), (1,)), ((), ()))
TN = (((0,), (0,)), ((), ()))
NN = (((1,), (0,)), ((), ()))

VMEM = pl.BlockSpec(memory_space=pltpu.VMEM)
SMEM = pl.BlockSpec(memory_space=pltpu.SMEM)


def call(body, out_shape, n_in, scratch=(), smem=0, flops=0, moved=0, exps=0):
    outs = out_shape if isinstance(out_shape, (tuple, list)) else None
    return pl.pallas_call(
        body,
        out_shape=out_shape,
        in_specs=[SMEM] * smem + [VMEM] * n_in,
        out_specs=[VMEM] * len(outs) if outs else VMEM,
        scratch_shapes=list(scratch),
        compiler_params=pltpu.CompilerParams(vmem_limit_bytes=24 * 2**20),
        cost_estimate=pl.CostEstimate(flops=flops, bytes_accessed=moved, transcendentals=exps),
    )


def dot(a, b, dims):
    return lax.dot_general(a, b, dims, preferred_element_type=F32)


def low_lanes(shape):
    return lax.broadcasted_iota(jnp.int32, shape, len(shape) - 1) < 64


def pack_memory(k_ref, v_ref, out_ref):
    low = low_lanes((BLOCK, 128))
    for t in range(HEADS // 2):
        k = k_ref[:, 128 * t : 128 * t + 128].astype(F32)
        v = v_ref[:, 128 * t : 128 * t + 128].astype(F32)
        out_ref[2 * t] = jnp.where(low, k, pltpu.roll(v, 64, 1)).astype(BF16)
        out_ref[2 * t + 1] = jnp.where(low, pltpu.roll(k, 64, 1), v).astype(BF16)


def pack_query(at_ref, q_ref, g_ref, out_ref):
    y, c = at_ref[0], at_ref[1]
    low = low_lanes((MINE, 128))
    for x in range(NX):
        lanes = pl.ds(pl.multiple_of((x * NY + y) * 128, 128), 128)
        q = q_ref[:, lanes].astype(F32)
        g = g_ref[:, lanes].astype(F32)
        first = jnp.where(low, q, pltpu.roll(g, 64, 1))
        second = jnp.where(low, pltpu.roll(q, 64, 1), g)
        out_ref[x] = jnp.where(c == 0, first, second).astype(BF16)


def halves(qg_ref):
    qg = qg_ref[...]
    low = low_lanes(qg.shape)
    zero = jnp.zeros_like(qg)
    return jnp.where(low, qg, zero), jnp.where(low, zero, qg)


def local_stats(kv_ref, qg_ref, out_ref, s_ref):
    q, g = halves(qg_ref)
    peak = None
    for j in range(0, MEMS, STEP):
        s = dot(kv_ref[j : j + STEP, :], q, NT)
        s_ref[j : j + STEP, :] = s
        top = jnp.max(s, axis=0, keepdims=True)
        peak = top if peak is None else jnp.maximum(peak, top)
    total = jnp.zeros((1, ROWS), F32)
    weighted = jnp.zeros((1, ROWS), F32)
    for j in range(0, MEMS, STEP):
        e = jnp.exp(s_ref[j : j + STEP, :] - peak)
        w = e * dot(kv_ref[j : j + STEP, :], g, NT)
        total += jnp.sum(e, axis=0, keepdims=True)
        weighted += jnp.sum(w, axis=0, keepdims=True)
    lse = peak + jnp.log(total)
    mean = weighted / total
    for d in range(NZ):
        for t in range(3):
            out_ref[d, t : t + 1, :] = lse[:, 128 * t : 128 * t + 128]
            out_ref[d, 4 + t : 5 + t, :] = mean[:, 128 * t : 128 * t + 128]


def whole_stats(st_ref):
    logs, offsets = [], []
    for t in range(3):
        part = st_ref[:, t, :]
        mean = st_ref[:, 4 + t, :]
        peak = jnp.max(part, axis=0, keepdims=True)
        e = jnp.exp(part - peak)
        total = jnp.sum(e, axis=0, keepdims=True)
        logs.append(peak + jnp.log(total))
        offsets.append(jnp.sum(e * mean, axis=0, keepdims=True) / total)
    return jnp.concatenate(logs, axis=1), jnp.concatenate(offsets, axis=1)


def query_part(st_ref, kv_ref, qg_ref, out_ref, ds_ref):
    lse, offset = whole_stats(st_ref)
    q, g = halves(qg_ref)
    for j in range(0, MEMS, STEP):
        kv = kv_ref[j : j + STEP, :]
        prob = jnp.exp(dot(kv, q, NT) - lse)
        ds_ref[j : j + STEP, :] = (prob * (dot(kv, g, NT) - offset)).astype(BF16)
    turned = dot(kv_ref[...], ds_ref[...], TN)
    dq = turned.T
    low = low_lanes((8, 128))
    for x in range(NX):
        for z in range(NZ):
            a = MINE * x + 8 * z
            b = MINE * x + 64 + 8 * (z // 2)
            out_ref[z * NX + x] = jnp.where(low, dq[a : a + 8, :], pltpu.roll(dq[b : b + 8, :], 64, 1))


def memory_grads(st_ref, kv_ref, qg_ref, out_ref):
    lse, offset = whole_stats(st_ref)
    q, g = halves(qg_ref)
    for j in range(0, MEMS, STEP):
        kv = kv_ref[j : j + STEP, :]
        prob = jnp.exp(dot(kv, q, NT) - lse)
        ds = (prob * (dot(kv, g, NT) - offset)).astype(BF16)
        out = dot(ds, q, NN) + dot(prob.astype(BF16), g, NN)
        out_ref[j : j + STEP, :] = out.astype(BF16)


def add_query(at_ref, in_ref, out_ref):
    odd = at_ref[0] % 2 == 1
    low = low_lanes((8, 128))
    top = lax.broadcasted_iota(jnp.int32, (8, 128), 0) < 4
    t = []
    for x in range(NX):
        total = in_ref[x]
        for z in range(1, NZ):
            total = total + in_ref[z * NX + x]
        t.append(total)
    full = [jnp.where(low, t[2 * p], pltpu.roll(t[2 * p + 1], 64, 1)) for p in range(2)]
    half = [jnp.where(low, pltpu.roll(t[2 * p], 64, 1), t[2 * p + 1]) for p in range(2)]
    even_half = jnp.where(top, half[0], pltpu.roll(half[1], 4, 0))
    odd_half = jnp.where(top, pltpu.roll(half[0], 4, 0), half[1])
    last = jnp.where(odd, odd_half, even_half)
    piece = jnp.concatenate([full[0], full[1], last], axis=0).astype(BF16)
    out_ref[...] = jnp.broadcast_to(piece[None], out_ref.shape)


def join_query(in_ref, out_ref):
    low = low_lanes((8, 128))
    top = lax.broadcasted_iota(jnp.int32, (8, 128), 0) < 4
    for y in range(NY):

        def heads(f0, f1):
            return jnp.where(low, f0, pltpu.roll(f1, 64, 1)), jnp.where(low, pltpu.roll(f0, 64, 1), f1)

        for z4 in range(0, NZ, 4):
            pieces = [[in_ref[c, z4 + i, y].astype(F32) for i in range(4)] for c in range(NC)]
            for p in range(2):
                tiles = [heads(pieces[0][i][8 * p : 8 * p + 8], pieces[1][i][8 * p : 8 * p + 8]) for i in range(4)]
                ends = []
                for i in (0, 2):
                    g = []
                    for c in range(NC):
                        even, odd = pieces[c][i][16:24], pieces[c][i + 1][16:24]
                        if p == 0:
                            g.append(jnp.where(top, even, pltpu.roll(odd, 4, 0)))
                        else:
                            g.append(jnp.where(top, pltpu.roll(even, 4, 0), odd))
                    ends.append(heads(g[0], g[1]))
                for u in range(2):
                    lanes = slice(((2 * p + u) * NY + y) * 128, ((2 * p + u) * NY + y) * 128 + 128)
                    for i in (0, 2):
                        r = 8 * (z4 + i)
                        both = jnp.concatenate([tiles[i][u], tiles[i + 1][u]], axis=0)
                        out_ref[r : r + 16, lanes] = both.astype(BF16)
                    r = 64 + 4 * z4
                    both = jnp.concatenate([ends[0][u], ends[1][u]], axis=0)
                    out_ref[r : r + 16, lanes] = both.astype(BF16)


def unpack_memory(in_ref, k_ref, v_ref):
    low = low_lanes((BLOCK, 128))
    for t in range(HEADS // 2):
        a = in_ref[2 * t].astype(F32)
        b = in_ref[2 * t + 1].astype(F32)
        k_ref[:, 128 * t : 128 * t + 128] = jnp.where(low, a, pltpu.roll(b, 64, 1)).astype(BF16)
        v_ref[:, 128 * t : 128 * t + 128] = jnp.where(low, pltpu.roll(a, 64, 1), b).astype(BF16)


def local(query, out_grad, keys, values):
    shape = jax.ShapeDtypeStruct
    z, y, c = lax.axis_index("z"), lax.axis_index("y"), lax.axis_index("core")
    at = jnp.stack([y, c]).astype(jnp.int32)
    zs = jnp.stack([z, c]).astype(jnp.int32)
    mega = 2**20

    memory = call(pack_memory, shape((HEADS, BLOCK, 128), BF16), 2, moved=mega)(keys, values)
    memory = lax.all_to_all(memory, ("y", "core"), 0, 0, tiled=True).reshape(MEMS, 128)
    pairs = call(pack_query, shape((NX, MINE, 128), BF16), 2, smem=1, moved=mega)(at, query, out_grad)
    pairs = lax.all_to_all(pairs, "row", 0, 0, tiled=True).reshape(ROWS, 128)

    work = 2 * MEMS * ROWS * 128
    stats = call(
        local_stats,
        shape((NZ, 8, 128), F32),
        2,
        scratch=[pltpu.VMEM((MEMS, ROWS), F32)],
        flops=2 * work,
        moved=mega,
        exps=MEMS * ROWS,
    )(memory, pairs)
    stats = lax.all_to_all(stats, "z", 0, 0, tiled=True)

    part = call(
        query_part,
        shape((NZ * NX, 8, 128), F32),
        3,
        scratch=[pltpu.VMEM((MEMS, ROWS), BF16)],
        flops=3 * work,
        moved=mega,
        exps=MEMS * ROWS,
    )(stats, memory, pairs)
    part = lax.all_to_all(part, ("z", "row"), 0, 0, tiled=True)
    grads = call(memory_grads, shape((MEMS, 128), BF16), 3, flops=4 * work, moved=mega, exps=MEMS * ROWS)(
        stats, memory, pairs
    )
    piece = call(add_query, shape((NZ * NY, 24, 128), BF16), 1, smem=1, moved=mega)(zs, part)
    piece = lax.all_to_all(piece, ("z", "y"), 0, 0, tiled=True).reshape(NZ, NY, 24, 128)
    pieces = lax.all_gather(piece, "core", axis=0, tiled=False)
    query_grad = call(join_query, shape((MINE, 4096), BF16), 1, moved=2 * mega)(pieces)

    grads = lax.all_to_all(grads.reshape(HEADS, BLOCK, 128), ("y", "core"), 0, 0, tiled=True)
    key_grad, value_grad = call(
        unpack_memory, [shape((BLOCK, 1024), BF16), shape((BLOCK, 1024), BF16)], 1, moved=mega
    )(grads)
    return (query_grad, key_grad, value_grad)


def solution(mesh):
    fine = Mesh(mesh.devices.reshape(NZ, NY, NC, NX), ("z", "y", "core", "row"))
    psg = ("z", "y", "core")
    placed = (P("row", None), P("row", None), P(psg, "row"), P(psg, "row"))
    return jax.shard_map(
        local,
        mesh=fine,
        in_specs=placed,
        out_specs=(P("row", None), P(psg, "row"), P(psg, "row")),
        check_vma=False,
    )
```

```python
import jax
import jax.numpy as jnp
from jax import lax
from jax.experimental import pallas as pl
from jax.experimental.pallas import tpu as pltpu
from jax.sharding import Mesh
from jax.sharding import PartitionSpec as P

F32 = jnp.float32
BF16 = jnp.bfloat16
NZ, NY, NC, NX = 8, 8, 2, 4
HEADS = 16
BLOCK = 128
ROWS = 384
MINE = ROWS // NX
MEMS = HEADS * BLOCK
STEP = 256
NT = (((1,), (1,)), ((), ()))
TN = (((0,), (0,)), ((), ()))
NN = (((1,), (0,)), ((), ()))

VMEM = pl.BlockSpec(memory_space=pltpu.VMEM)
SMEM = pl.BlockSpec(memory_space=pltpu.SMEM)


def call(body, out_shape, n_in, scratch=(), smem=0, flops=0, moved=0, exps=0):
    outs = out_shape if isinstance(out_shape, (tuple, list)) else None
    return pl.pallas_call(
        body,
        out_shape=out_shape,
        in_specs=[SMEM] * smem + [VMEM] * n_in,
        out_specs=[VMEM] * len(outs) if outs else VMEM,
        scratch_shapes=list(scratch),
        compiler_params=pltpu.CompilerParams(vmem_limit_bytes=40 * 2**20),
        cost_estimate=pl.CostEstimate(flops=flops, bytes_accessed=moved, transcendentals=exps),
    )


def dot(a, b, dims):
    return lax.dot_general(a, b, dims, preferred_element_type=F32)


def low_lanes(shape):
    return lax.broadcasted_iota(jnp.int32, shape, len(shape) - 1) < 64


def pack_memory(k_ref, v_ref, out_ref):
    low = low_lanes((BLOCK, 128))
    for t in range(HEADS // 2):
        k = k_ref[:, 128 * t : 128 * t + 128].astype(F32)
        v = v_ref[:, 128 * t : 128 * t + 128].astype(F32)
        out_ref[2 * t] = jnp.where(low, k, pltpu.roll(v, 64, 1)).astype(BF16)
        out_ref[2 * t + 1] = jnp.where(low, pltpu.roll(k, 64, 1), v).astype(BF16)


def pack_query(at_ref, q_ref, g_ref, *outs):
    x, y, c = at_ref[0], at_ref[1], at_ref[2]
    low = low_lanes((MINE, 128))
    for k in range(NX):
        lanes = pl.ds(pl.multiple_of((lax.rem(x + k, NX) * NY + y) * 128, 128), 128)
        q = q_ref[:, lanes].astype(F32)
        g = g_ref[:, lanes].astype(F32)
        first = jnp.where(low, q, pltpu.roll(g, 64, 1))
        second = jnp.where(low, pltpu.roll(q, 64, 1), g)
        outs[k][...] = jnp.where(c == 0, first, second).astype(BF16)


def pack_all_heads(at_ref, q_ref, g_ref, *outs):
    x = at_ref[0]
    low = low_lanes((MINE, 128))
    for k in range(NX):
        start = lax.rem(x + k, NX) * 1024
        for t in range(HEADS // 2):
            lanes = pl.ds(pl.multiple_of(start + 128 * t, 128), 128)
            q = q_ref[:, lanes].astype(F32)
            g = g_ref[:, lanes].astype(F32)
            outs[k][2 * t] = jnp.where(low, q, pltpu.roll(g, 64, 1)).astype(BF16)
            outs[k][2 * t + 1] = jnp.where(low, pltpu.roll(q, 64, 1), g).astype(BF16)


def halves(qg):
    low = low_lanes(qg.shape)
    zero = jnp.zeros_like(qg)
    return jnp.where(low, qg, zero), jnp.where(low, zero, qg)


def local_part(at_ref, kv_ref, q0, q1, q2, q3, out_ref, e_ref, gp_ref, ds_ref, p_ref):
    x = at_ref[0]
    q, g = halves(jnp.concatenate([q0[...], q1[...], q2[...], q3[...]], axis=0))
    peak = None
    for j in range(0, MEMS, STEP):
        s = dot(kv_ref[j : j + STEP, :], q, NT)
        e_ref[j : j + STEP, :] = s
        top = jnp.max(s, axis=0, keepdims=True)
        peak = top if peak is None else jnp.maximum(peak, top)
    total = jnp.zeros((1, ROWS), F32)
    weighted = jnp.zeros((1, ROWS), F32)
    for j in range(0, MEMS, STEP):
        e = jnp.exp(e_ref[j : j + STEP, :] - peak)
        e_ref[j : j + STEP, :] = e
        gp = dot(kv_ref[j : j + STEP, :], g, NT)
        gp_ref[j : j + STEP, :] = gp
        total += jnp.sum(e, axis=0, keepdims=True)
        weighted += jnp.sum(e * gp, axis=0, keepdims=True)
    lse = peak + jnp.log(total)
    mean = weighted / total
    inverse = 1.0 / total
    for j in range(0, MEMS, STEP):
        prob = e_ref[j : j + STEP, :] * inverse
        p_ref[j : j + STEP, :] = prob.astype(BF16)
        ds_ref[j : j + STEP, :] = (prob * (gp_ref[j : j + STEP, :] - mean)).astype(BF16)
    kv = kv_ref[...]
    first = dot(kv, ds_ref[...], TN)[:64]
    second = dot(kv, p_ref[...], TN)[:64]
    both = jnp.concatenate([first, second], axis=0).T
    pad = jnp.zeros((1, 128 - MINE), F32)
    for r in range(NX):
        owner = lax.rem(x - r + NX, NX)
        own = [jnp.concatenate([a[:, MINE * r : MINE * r + MINE], pad], axis=1) for a in (lse, mean)]
        for z in range(NZ):
            t = 128 * min(z, 2)
            a = MINE * r + 8 * z
            b = MINE * r + 64 + 4 * z
            out_ref[z * NX + owner, 0:8, :] = both[a : a + 8, :]
            rows = [both[b : b + 4, :], lse[:, t : t + 128], mean[:, t : t + 128]] + own
            out_ref[z * NX + owner, 8:16, :] = jnp.concatenate(rows, axis=0)


def weights(logs, means):
    peak = jnp.max(logs, axis=0, keepdims=True)
    e = jnp.exp(logs - peak)
    total = jnp.sum(e, axis=0, keepdims=True)
    w = e / total
    offset = jnp.sum(w * means, axis=0, keepdims=True)
    return peak + jnp.log(total), offset, w


def three(a):
    first = a.astype(BF16).astype(F32)
    second = (a - first).astype(BF16).astype(F32)
    return [first, second, a - first - second]


def add_query(at_ref, in_ref, out_ref, col_ref):
    z, x = at_ref[0], at_ref[1]
    odd = lax.rem(z, 2) == 1
    low = low_lanes((8, 128))
    top = lax.broadcasted_iota(jnp.int32, (8, 128), 0) < 4
    full, half = [], []
    for u in range(NX):
        logs = jnp.concatenate([in_ref[d * NX + u, 14:15, :] for d in range(NZ)], axis=0)
        means = jnp.concatenate([in_ref[d * NX + u, 15:16, :] for d in range(NZ)], axis=0)
        _, offset, w = weights(logs, means)
        shift = w * (means - offset)
        col_ref[u] = jnp.concatenate([w, shift, jnp.zeros((112, 128), F32)], axis=0).T
        cols = col_ref[u, pl.ds(pl.multiple_of(8 * z, 8), 8), :]
        ends = col_ref[u, pl.ds(pl.multiple_of(64 + 8 * (z // 2), 8), 8), :]
        ends = jnp.where(odd, pltpu.roll(ends, 4, 0), ends)
        a = jnp.zeros((8, 128), F32)
        b = jnp.zeros((8, 128), F32)
        for d in range(NZ):
            tile = in_ref[d * NX + u]
            a += tile[0:8] * jnp.where(low, cols[:, d : d + 1], cols[:, 8 + d : 9 + d])
            b += tile[8:16] * jnp.where(low, ends[:, d : d + 1], ends[:, 8 + d : 9 + d])
        full.append(a + pltpu.roll(a, 64, 1))
        half.append(b + pltpu.roll(b, 64, 1))
    f = [jnp.where(low, full[2 * p], full[2 * p + 1]) for p in range(2)]
    h = [jnp.where(low, half[2 * p], half[2 * p + 1]) for p in range(2)]
    logs = jnp.concatenate([in_ref[d * NX + x, 12:13, :] for d in range(NZ)], axis=0)
    means = jnp.concatenate([in_ref[d * NX + x, 13:14, :] for d in range(NZ)], axis=0)
    lse, offset, _ = weights(logs, means)
    stats = three(lse) + three(offset) + [jnp.zeros((2, 128), F32)]
    piece = jnp.concatenate([f[0], f[1], jnp.where(top, h[0], pltpu.roll(h[1], 4, 0))] + stats, axis=0)
    out_ref[...] = jnp.broadcast_to(piece.astype(BF16)[None], out_ref.shape)


def join_query(in_ref, out_ref):
    low = low_lanes((8, 128))
    top = lax.broadcasted_iota(jnp.int32, (8, 128), 0) < 4
    for y in range(NY):

        def heads(f0, f1):
            return jnp.where(low, f0, pltpu.roll(f1, 64, 1)), jnp.where(low, pltpu.roll(f0, 64, 1), f1)

        for z4 in range(0, NZ, 4):
            pieces = [[in_ref[c, z4 + i, y].astype(F32) for i in range(4)] for c in range(NC)]
            for p in range(2):
                tiles = [heads(pieces[0][i][8 * p : 8 * p + 8], pieces[1][i][8 * p : 8 * p + 8]) for i in range(4)]
                ends = []
                for i in (0, 2):
                    g = []
                    for c in range(NC):
                        even, odd = pieces[c][i][16:24], pieces[c][i + 1][16:24]
                        if p == 0:
                            g.append(jnp.where(top, even, pltpu.roll(odd, 4, 0)))
                        else:
                            g.append(jnp.where(top, pltpu.roll(even, 4, 0), odd))
                    ends.append(heads(g[0], g[1]))
                for u in range(2):
                    lanes = slice(((2 * p + u) * NY + y) * 128, ((2 * p + u) * NY + y) * 128 + 128)
                    for i in (0, 2):
                        r = 8 * (z4 + i)
                        both = jnp.concatenate([tiles[i][u], tiles[i + 1][u]], axis=0)
                        out_ref[r : r + 16, lanes] = both.astype(BF16)
                    r = 64 + 4 * z4
                    both = jnp.concatenate([ends[0][u], ends[1][u]], axis=0)
                    out_ref[r : r + 16, lanes] = both.astype(BF16)


def memory_grads(in_ref, kv_ref, q0, q1, q2, q3, k_ref, v_ref):
    low = low_lanes((BLOCK, 128))
    for y in range(NY):
        outs = []
        for c in range(NC):
            h = y * NC + c
            logs, offsets = [], []
            for t in range(3):
                piece = in_ref[c, t, y].astype(F32)
                logs.append(piece[24:25] + piece[25:26] + piece[26:27])
                offsets.append(piece[27:28] + piece[28:29] + piece[29:30])
            lse = jnp.concatenate(logs, axis=1)
            offset = jnp.concatenate(offsets, axis=1)
            q, g = halves(jnp.concatenate([q0[h], q1[h], q2[h], q3[h]], axis=0))
            kv = kv_ref[h]
            prob = jnp.exp(dot(kv, q, NT) - lse)
            ds = (prob * (dot(kv, g, NT) - offset)).astype(BF16)
            outs.append(dot(ds, q, NN) + dot(prob.astype(BF16), g, NN))
        a, b = outs
        lanes = slice(128 * y, 128 * y + 128)
        k_ref[:, lanes] = jnp.where(low, a, pltpu.roll(b, 64, 1)).astype(BF16)
        v_ref[:, lanes] = jnp.where(low, pltpu.roll(a, 64, 1), b).astype(BF16)


def around(parts):
    return parts[:1] + [
        lax.ppermute(parts[k], "row", [(i, (i + k) % NX) for i in range(NX)]) for k in range(1, NX)
    ]


def local(query, out_grad, keys, values):
    shape = jax.ShapeDtypeStruct
    z, y, c = lax.axis_index("z"), lax.axis_index("y"), lax.axis_index("core")
    x = lax.axis_index("row")
    at = jnp.stack([x, y, c]).astype(jnp.int32)
    zx = jnp.stack([z, x]).astype(jnp.int32)
    mega = 2**20

    home = call(pack_memory, shape((HEADS, BLOCK, 128), BF16), 2, moved=mega)(keys, values)
    memory = lax.all_to_all(home, ("y", "core"), 0, 0, tiled=True).reshape(MEMS, 128)
    mine = call(pack_query, [shape((MINE, 128), BF16)] * NX, 2, smem=1, moved=mega)(at, query, out_grad)
    mine = around(list(mine))
    every = call(pack_all_heads, [shape((HEADS, MINE, 128), BF16)] * NX, 2, smem=1, moved=3 * mega)(
        at, query, out_grad
    )
    every = around(list(every))

    work = 2 * MEMS * ROWS * 128
    part = call(
        local_part,
        shape((NZ * NX, 16, 128), F32),
        5,
        smem=1,
        scratch=[pltpu.VMEM((MEMS, ROWS), F32)] * 2 + [pltpu.VMEM((MEMS, ROWS), BF16)] * 2,
        flops=4 * work,
        moved=mega,
        exps=MEMS * ROWS,
    )(at, memory, *mine)
    part = lax.all_to_all(part, ("z", "row"), 0, 0, tiled=True)
    piece = call(
        add_query,
        shape((NZ * NY, 32, 128), BF16),
        1,
        smem=1,
        scratch=[pltpu.VMEM((NX, 128, 128), F32)],
        moved=mega,
    )(zx, part)
    piece = lax.all_to_all(piece, ("z", "y"), 0, 0, tiled=True).reshape(NZ, NY, 32, 128)
    pieces = lax.all_gather(piece, "core", axis=0, tiled=False)
    query_grad = call(join_query, shape((MINE, 4096), BF16), 1, moved=2 * mega)(pieces)
    key_grad, value_grad = call(
        memory_grads,
        [shape((BLOCK, 1024), BF16), shape((BLOCK, 1024), BF16)],
        6,
        flops=4 * work,
        moved=3 * mega,
        exps=MEMS * ROWS,
    )(pieces, home, *every)
    return (query_grad, key_grad, value_grad)


def solution(mesh):
    fine = Mesh(mesh.devices.reshape(NZ, NY, NC, NX), ("z", "y", "core", "row"))
    psg = ("z", "y", "core")
    placed = (P("row", None), P("row", None), P(psg, "row"), P(psg, "row"))
    return jax.shard_map(
        local,
        mesh=fine,
        in_specs=placed,
        out_specs=(P("row", None), P(psg, "row"), P(psg, "row")),
        check_vma=False,
    )
```

```python
import jax
import jax.numpy as jnp
from jax import lax
from jax.experimental import pallas as pl
from jax.experimental.pallas import tpu as pltpu
from jax.sharding import Mesh
from jax.sharding import PartitionSpec as P

F32 = jnp.float32
BF16 = jnp.bfloat16
NZ, NY, NC, NX = 8, 8, 2, 4
HEADS = 16
BLOCK = 128
ROWS = 384
MINE = ROWS // NX
MEMS = HEADS * BLOCK
STEP = 256
NT = (((1,), (1,)), ((), ()))
TN = (((0,), (0,)), ((), ()))
SWAP = [(0, 1), (1, 0)]
NN = (((1,), (0,)), ((), ()))

VMEM = pl.BlockSpec(memory_space=pltpu.VMEM)
SMEM = pl.BlockSpec(memory_space=pltpu.SMEM)


def call(body, out_shape, n_in, scratch=(), smem=0, flops=0, moved=0, exps=0):
    outs = out_shape if isinstance(out_shape, (tuple, list)) else None
    return pl.pallas_call(
        body,
        out_shape=out_shape,
        in_specs=[SMEM] * smem + [VMEM] * n_in,
        out_specs=[VMEM] * len(outs) if outs else VMEM,
        scratch_shapes=list(scratch),
        compiler_params=pltpu.CompilerParams(vmem_limit_bytes=40 * 2**20),
        cost_estimate=pl.CostEstimate(flops=flops, bytes_accessed=moved, transcendentals=exps),
    )


def dot(a, b, dims):
    return lax.dot_general(a, b, dims, preferred_element_type=F32)


def low_lanes(shape):
    return lax.broadcasted_iota(jnp.int32, shape, len(shape) - 1) < 64


def pack_memory(k_ref, v_ref, out_ref):
    low = low_lanes((BLOCK, 128))
    for t in range(HEADS // 2):
        k = k_ref[:, 128 * t : 128 * t + 128].astype(F32)
        v = v_ref[:, 128 * t : 128 * t + 128].astype(F32)
        out_ref[2 * t] = jnp.where(low, k, pltpu.roll(v, 64, 1)).astype(BF16)
        out_ref[2 * t + 1] = jnp.where(low, pltpu.roll(k, 64, 1), v).astype(BF16)


def pack_query(at_ref, q_ref, g_ref, *outs):
    x, c = at_ref[0], at_ref[2]
    low = low_lanes((MINE, 128))
    for k in range(NX):
        start = lax.rem(x + k, NX) * 1024
        for t in range(HEADS // 2):
            lanes = pl.ds(pl.multiple_of(start + 128 * t, 128), 128)
            q = q_ref[:, lanes].astype(F32)
            g = g_ref[:, lanes].astype(F32)
            first = jnp.where(low, q, pltpu.roll(g, 64, 1))
            second = jnp.where(low, pltpu.roll(q, 64, 1), g)
            outs[k][t] = jnp.where(c == 0, first, second).astype(BF16)
            if k == 0:
                outs[NX][t] = jnp.where(c == 0, second, first).astype(BF16)


def halves(qg):
    low = low_lanes(qg.shape)
    zero = jnp.zeros_like(qg)
    return jnp.where(low, qg, zero), jnp.where(low, zero, qg)


def local_part(at_ref, kv_ref, q0, q1, q2, q3, out_ref, e_ref, gp_ref, ds_ref, p_ref):
    x, y = at_ref[0], at_ref[1]
    q, g = halves(jnp.concatenate([q0[y], q1[y], q2[y], q3[y]], axis=0))
    peak = None
    for j in range(0, MEMS, STEP):
        s = dot(kv_ref[j : j + STEP, :], q, NT)
        e_ref[j : j + STEP, :] = s
        top = jnp.max(s, axis=0, keepdims=True)
        peak = top if peak is None else jnp.maximum(peak, top)
    total = jnp.zeros((1, ROWS), F32)
    weighted = jnp.zeros((1, ROWS), F32)
    for j in range(0, MEMS, STEP):
        e = jnp.exp(e_ref[j : j + STEP, :] - peak)
        e_ref[j : j + STEP, :] = e
        gp = dot(kv_ref[j : j + STEP, :], g, NT)
        gp_ref[j : j + STEP, :] = gp
        total += jnp.sum(e, axis=0, keepdims=True)
        weighted += jnp.sum(e * gp, axis=0, keepdims=True)
    lse = peak + jnp.log(total)
    mean = weighted / total
    inverse = 1.0 / total
    for j in range(0, MEMS, STEP):
        prob = e_ref[j : j + STEP, :] * inverse
        p_ref[j : j + STEP, :] = prob.astype(BF16)
        ds_ref[j : j + STEP, :] = (prob * (gp_ref[j : j + STEP, :] - mean)).astype(BF16)
    kv = kv_ref[...]
    first = dot(kv, ds_ref[...], TN)[:64]
    second = dot(kv, p_ref[...], TN)[:64]
    both = jnp.concatenate([first, second], axis=0).T
    pad = jnp.zeros((1, 128 - MINE), F32)
    for r in range(NX):
        owner = lax.rem(x - r + NX, NX)
        own = [jnp.concatenate([a[:, MINE * r : MINE * r + MINE], pad], axis=1) for a in (lse, mean)]
        for z in range(NZ):
            t = 128 * min(z, 2)
            a = MINE * r + 8 * z
            b = MINE * r + 64 + 4 * z
            out_ref[z * NX + owner, 0:8, :] = both[a : a + 8, :]
            rows = [both[b : b + 4, :], lse[:, t : t + 128], mean[:, t : t + 128]] + own
            out_ref[z * NX + owner, 8:16, :] = jnp.concatenate(rows, axis=0)


def weights(logs, means):
    peak = jnp.max(logs, axis=0, keepdims=True)
    e = jnp.exp(logs - peak)
    total = jnp.sum(e, axis=0, keepdims=True)
    w = e / total
    offset = jnp.sum(w * means, axis=0, keepdims=True)
    return peak + jnp.log(total), offset, w


def three(a):
    first = a.astype(BF16).astype(F32)
    second = (a - first).astype(BF16).astype(F32)
    return [first, second, a - first - second]


def add_query(at_ref, in_ref, out_ref, col_ref):
    z, x = at_ref[0], at_ref[1]
    odd = lax.rem(z, 2) == 1
    low = low_lanes((8, 128))
    top = lax.broadcasted_iota(jnp.int32, (8, 128), 0) < 4
    full, half = [], []
    for u in range(NX):
        logs = jnp.concatenate([in_ref[d * NX + u, 14:15, :] for d in range(NZ)], axis=0)
        means = jnp.concatenate([in_ref[d * NX + u, 15:16, :] for d in range(NZ)], axis=0)
        _, offset, w = weights(logs, means)
        shift = w * (means - offset)
        col_ref[u] = jnp.concatenate([w, shift, jnp.zeros((112, 128), F32)], axis=0).T
        cols = col_ref[u, pl.ds(pl.multiple_of(8 * z, 8), 8), :]
        ends = col_ref[u, pl.ds(pl.multiple_of(64 + 8 * (z // 2), 8), 8), :]
        ends = jnp.where(odd, pltpu.roll(ends, 4, 0), ends)
        a = jnp.zeros((8, 128), F32)
        b = jnp.zeros((8, 128), F32)
        for d in range(NZ):
            tile = in_ref[d * NX + u]
            a += tile[0:8] * jnp.where(low, cols[:, d : d + 1], cols[:, 8 + d : 9 + d])
            b += tile[8:16] * jnp.where(low, ends[:, d : d + 1], ends[:, 8 + d : 9 + d])
        full.append(a + pltpu.roll(a, 64, 1))
        half.append(b + pltpu.roll(b, 64, 1))
    f = [jnp.where(low, full[2 * p], full[2 * p + 1]) for p in range(2)]
    h = [jnp.where(low, half[2 * p], half[2 * p + 1]) for p in range(2)]
    logs = jnp.concatenate([in_ref[d * NX + x, 12:13, :] for d in range(NZ)], axis=0)
    means = jnp.concatenate([in_ref[d * NX + x, 13:14, :] for d in range(NZ)], axis=0)
    lse, offset, _ = weights(logs, means)
    stats = three(lse) + three(offset) + [jnp.zeros((2, 128), F32)]
    piece = jnp.concatenate([f[0], f[1], jnp.where(top, h[0], pltpu.roll(h[1], 4, 0))] + stats, axis=0)
    out_ref[...] = jnp.broadcast_to(piece.astype(BF16)[None], out_ref.shape)


def by_core(at_ref, a, b):
    first = at_ref[0] == 0
    return jnp.where(first, a, b), jnp.where(first, b, a)


def join_query(at_ref, own_ref, other_ref, out_ref):
    low = low_lanes((8, 128))
    top = lax.broadcasted_iota(jnp.int32, (8, 128), 0) < 4
    for y in range(NY):

        def heads(f0, f1):
            return jnp.where(low, f0, pltpu.roll(f1, 64, 1)), jnp.where(low, pltpu.roll(f0, 64, 1), f1)

        for z4 in range(0, NZ, 4):
            where = [(z4 + i) * NY + y for i in range(4)]
            pairs = [by_core(at_ref, own_ref[w].astype(F32), other_ref[w].astype(F32)) for w in where]
            pieces = [[pairs[i][c] for i in range(4)] for c in range(NC)]
            for p in range(2):
                tiles = [heads(pieces[0][i][8 * p : 8 * p + 8], pieces[1][i][8 * p : 8 * p + 8]) for i in range(4)]
                ends = []
                for i in (0, 2):
                    g = []
                    for c in range(NC):
                        even, odd = pieces[c][i][16:24], pieces[c][i + 1][16:24]
                        if p == 0:
                            g.append(jnp.where(top, even, pltpu.roll(odd, 4, 0)))
                        else:
                            g.append(jnp.where(top, pltpu.roll(even, 4, 0), odd))
                    ends.append(heads(g[0], g[1]))
                for u in range(2):
                    lanes = slice(((2 * p + u) * NY + y) * 128, ((2 * p + u) * NY + y) * 128 + 128)
                    for i in (0, 2):
                        r = 8 * (z4 + i)
                        both = jnp.concatenate([tiles[i][u], tiles[i + 1][u]], axis=0)
                        out_ref[r : r + 16, lanes] = both.astype(BF16)
                    r = 64 + 4 * z4
                    both = jnp.concatenate([ends[0][u], ends[1][u]], axis=0)
                    out_ref[r : r + 16, lanes] = both.astype(BF16)


def head_grads(told_ref, y, kv, qs):
    logs, offsets = [], []
    for t in range(3):
        piece = told_ref[t * NY + y].astype(F32)
        logs.append(piece[24:25] + piece[25:26] + piece[26:27])
        offsets.append(piece[27:28] + piece[28:29] + piece[29:30])
    lse = jnp.concatenate(logs, axis=1)
    offset = jnp.concatenate(offsets, axis=1)
    q, g = halves(jnp.concatenate([q_ref[y] for q_ref in qs], axis=0))
    prob = jnp.exp(dot(kv, q, NT) - lse)
    ds = (prob * (dot(kv, g, NT) - offset)).astype(BF16)
    return dot(ds, q, NN) + dot(prob.astype(BF16), g, NN)


def own_grads(core_ref, told_ref, kv_ref, q0, q1, q2, q3, out_ref):
    c = core_ref[0]
    for y in range(NY):
        out_ref[y] = head_grads(told_ref, y, kv_ref[2 * y + c], (q0, q1, q2, q3)).astype(BF16)


def other_grads(core_ref, told_ref, kv_ref, q0, q1, q2, q3, own_ref, k_ref, v_ref):
    c = core_ref[0]
    low = low_lanes((BLOCK, 128))
    for y in range(NY):
        other = head_grads(told_ref, y, kv_ref[2 * y + 1 - c], (q0, q1, q2, q3))
        own = own_ref[y].astype(F32)
        a = jnp.where(c == 0, own, other)
        b = jnp.where(c == 0, other, own)
        lanes = slice(128 * y, 128 * y + 128)
        k_ref[:, lanes] = jnp.where(low, a, pltpu.roll(b, 64, 1)).astype(BF16)
        v_ref[:, lanes] = jnp.where(low, pltpu.roll(a, 64, 1), b).astype(BF16)


def around(parts):
    return parts[:1] + [
        lax.ppermute(parts[k], "row", [(i, (i + k) % NX) for i in range(NX)]) for k in range(1, NX)
    ]


def local(query, out_grad, keys, values):
    shape = jax.ShapeDtypeStruct
    z, y, c = lax.axis_index("z"), lax.axis_index("y"), lax.axis_index("core")
    x = lax.axis_index("row")
    at = jnp.stack([x, y, c]).astype(jnp.int32)
    zx = jnp.stack([z, x]).astype(jnp.int32)
    corez = c.astype(jnp.int32)[None]
    mega = 2**20

    home = call(pack_memory, shape((HEADS, BLOCK, 128), BF16), 2, moved=mega)(keys, values)
    memory = lax.all_to_all(home, ("y", "core"), 0, 0, tiled=True).reshape(MEMS, 128)
    *mine, rest = call(pack_query, [shape((NY, MINE, 128), BF16)] * (NX + 1), 2, smem=1, moved=3 * mega)(
        at, query, out_grad
    )
    mine = around(mine)
    rest = [rest] + [lax.ppermute(a, "core", SWAP) for a in mine[1:]]

    work = 2 * MEMS * ROWS * 128
    part = call(
        local_part,
        shape((NZ * NX, 16, 128), F32),
        5,
        smem=1,
        scratch=[pltpu.VMEM((MEMS, ROWS), F32)] * 2 + [pltpu.VMEM((MEMS, ROWS), BF16)] * 2,
        flops=4 * work,
        moved=mega,
        exps=MEMS * ROWS,
    )(at, memory, *mine)
    part = lax.all_to_all(part, ("z", "row"), 0, 0, tiled=True)
    piece = call(
        add_query,
        shape((NZ * NY, 32, 128), BF16),
        1,
        smem=1,
        scratch=[pltpu.VMEM((NX, 128, 128), F32)],
        moved=mega,
    )(zx, part)
    piece, *rest = lax.optimization_barrier((piece, *rest))
    piece = lax.all_to_all(piece, ("z", "y"), 0, 0, tiled=True)
    other = lax.ppermute(piece, "core", SWAP)
    query_grad = call(join_query, shape((MINE, 4096), BF16), 2, smem=1, moved=2 * mega)(corez, piece, other)
    own = call(own_grads, shape((NY, BLOCK, 128), BF16), 6, smem=1, flops=2 * work, moved=mega, exps=MEMS * ROWS)(
        corez, piece, home, *mine
    )
    key_grad, value_grad = call(
        other_grads,
        [shape((BLOCK, 1024), BF16), shape((BLOCK, 1024), BF16)],
        7,
        smem=1,
        flops=2 * work,
        moved=2 * mega,
        exps=MEMS * ROWS,
    )(corez, other, home, *rest, own)
    return (query_grad, key_grad, value_grad)


def solution(mesh):
    fine = Mesh(mesh.devices.reshape(NZ, NY, NC, NX), ("z", "y", "core", "row"))
    psg = ("z", "y", "core")
    placed = (P("row", None), P("row", None), P(psg, "row"), P(psg, "row"))
    return jax.shard_map(
        local,
        mesh=fine,
        in_specs=placed,
        out_specs=(P("row", None), P(psg, "row"), P(psg, "row")),
        check_vma=False,
    )
```

```python
import jax
import jax.numpy as jnp
from jax import lax
from jax.experimental import pallas as pl
from jax.experimental.pallas import tpu as pltpu
from jax.sharding import Mesh
from jax.sharding import PartitionSpec as P

F32 = jnp.float32
BF16 = jnp.bfloat16
NZ, NY, NC, NX = 8, 8, 2, 4
HEADS = 16
BLOCK = 128
ROWS = 384
MINE = ROWS // NX
MEMS = HEADS * BLOCK
STEP = 256
NT = (((1,), (1,)), ((), ()))
TN = (((0,), (0,)), ((), ()))
SWAP = [(0, 1), (1, 0)]
NN = (((1,), (0,)), ((), ()))

VMEM = pl.BlockSpec(memory_space=pltpu.VMEM)
SMEM = pl.BlockSpec(memory_space=pltpu.SMEM)


def call(body, out_shape, n_in, scratch=(), smem=0, flops=0, moved=0, exps=0):
    outs = out_shape if isinstance(out_shape, (tuple, list)) else None
    return pl.pallas_call(
        body,
        out_shape=out_shape,
        in_specs=[SMEM] * smem + [VMEM] * n_in,
        out_specs=[VMEM] * len(outs) if outs else VMEM,
        scratch_shapes=list(scratch),
        compiler_params=pltpu.CompilerParams(vmem_limit_bytes=24 * 2**20),
        cost_estimate=pl.CostEstimate(flops=flops, bytes_accessed=moved, transcendentals=exps),
    )


def fetching(body, out_shape, n_in, scratch):
    return pl.pallas_call(
        body,
        out_shape=out_shape,
        in_specs=[SMEM] + [pl.BlockSpec(memory_space=pl.ANY)] * n_in,
        out_specs=[VMEM] * len(out_shape),
        scratch_shapes=scratch,
        compiler_params=pltpu.CompilerParams(vmem_limit_bytes=60 * 2**20),
        cost_estimate=pl.CostEstimate(flops=0, bytes_accessed=2**20, transcendentals=0),
    )


def dot(a, b, dims):
    return lax.dot_general(a, b, dims, preferred_element_type=F32)


def low_lanes(shape):
    return lax.broadcasted_iota(jnp.int32, shape, len(shape) - 1) < 64


def pack_memory(core_ref, k_hbm, v_hbm, out_ref, own_ref, away_ref, k_ref, v_ref, sems):
    c = core_ref[0]
    low = low_lanes((BLOCK, 128))
    copies = []
    for i in range(2):
        lanes = pl.ds(512 * i, 512)
        copies.append(pltpu.make_async_copy(k_hbm.at[:, lanes], k_ref.at[:, lanes], sems.at[0, i]))
        copies.append(pltpu.make_async_copy(v_hbm.at[:, lanes], v_ref.at[:, lanes], sems.at[1, i]))
    for copy in copies:
        copy.start()
    for t in range(HEADS // 2):
        if t % 4 == 0:
            copies[t // 2].wait()
            copies[t // 2 + 1].wait()
        k = k_ref[:, 128 * t : 128 * t + 128].astype(F32)
        v = v_ref[:, 128 * t : 128 * t + 128].astype(F32)
        first = jnp.where(low, k, pltpu.roll(v, 64, 1))
        second = jnp.where(low, pltpu.roll(k, 64, 1), v)
        out_ref[2 * t] = first.astype(BF16)
        out_ref[2 * t + 1] = second.astype(BF16)
        own_ref[t] = jnp.where(c == 0, first, second).astype(BF16)
        away_ref[t] = jnp.where(c == 0, second, first).astype(BF16)


def pack_mine(at_ref, q_ref, g_ref, *outs):
    x, y, c = at_ref[0], at_ref[1], at_ref[2]
    low = low_lanes((MINE, 128))
    for k in range(NX):
        lanes = pl.ds(pl.multiple_of((lax.rem(x + k, NX) * NY + y) * 128, 128), 128)
        q = q_ref[:, lanes].astype(F32)
        g = g_ref[:, lanes].astype(F32)
        first = jnp.where(low, q, pltpu.roll(g, 64, 1))
        second = jnp.where(low, pltpu.roll(q, 64, 1), g)
        outs[k][...] = jnp.where(c == 0, first, second).astype(BF16)


def pack_query(at_ref, q_ref, g_ref, *outs):
    x, c = at_ref[0], at_ref[2]
    low = low_lanes((MINE, 128))
    for k in range(NX):
        start = lax.rem(x + k, NX) * 1024
        for t in range(HEADS // 2):
            lanes = pl.ds(pl.multiple_of(start + 128 * t, 128), 128)
            q = q_ref[:, lanes].astype(F32)
            g = g_ref[:, lanes].astype(F32)
            first = jnp.where(low, q, pltpu.roll(g, 64, 1))
            second = jnp.where(low, pltpu.roll(q, 64, 1), g)
            outs[k][t] = jnp.where(c == 0, first, second).astype(BF16)


def halves(qg):
    low = low_lanes(qg.shape)
    zero = jnp.zeros_like(qg)
    return jnp.where(low, qg, zero), jnp.where(low, zero, qg)


def local_part(at_ref, kv_ref, q0, q1, q2, q3, out_ref, e_ref, gp_ref, ds_ref, p_ref):
    x = at_ref[0]
    q, g = halves(jnp.concatenate([q0[...], q1[...], q2[...], q3[...]], axis=0))
    peak = None
    for j in range(0, MEMS, STEP):
        s = dot(kv_ref[j : j + STEP, :], q, NT)
        e_ref[j : j + STEP, :] = s
        top = jnp.max(s, axis=0, keepdims=True)
        peak = top if peak is None else jnp.maximum(peak, top)
    total = jnp.zeros((1, ROWS), F32)
    weighted = jnp.zeros((1, ROWS), F32)
    for j in range(0, MEMS, STEP):
        e = jnp.exp(e_ref[j : j + STEP, :] - peak)
        e_ref[j : j + STEP, :] = e
        gp = dot(kv_ref[j : j + STEP, :], g, NT)
        gp_ref[j : j + STEP, :] = gp
        total += jnp.sum(e, axis=0, keepdims=True)
        weighted += jnp.sum(e * gp, axis=0, keepdims=True)
    lse = peak + jnp.log(total)
    mean = weighted / total
    inverse = 1.0 / total
    for j in range(0, MEMS, STEP):
        prob = e_ref[j : j + STEP, :] * inverse
        p_ref[j : j + STEP, :] = prob.astype(BF16)
        ds_ref[j : j + STEP, :] = (prob * (gp_ref[j : j + STEP, :] - mean)).astype(BF16)
    kv = kv_ref[...]
    first = dot(kv, ds_ref[...], TN)[:64]
    second = dot(kv, p_ref[...], TN)[:64]
    both = jnp.concatenate([first, second], axis=0).T
    pad = jnp.zeros((1, 128 - MINE), F32)
    for r in range(NX):
        owner = lax.rem(x - r + NX, NX)
        own = [jnp.concatenate([a[:, MINE * r : MINE * r + MINE], pad], axis=1) for a in (lse, mean)]
        for z in range(NZ):
            t = 128 * min(z, 2)
            a = MINE * r + 8 * z
            b = MINE * r + 64 + 4 * z
            out_ref[z * NX + owner, 0:8, :] = both[a : a + 8, :]
            rows = [both[b : b + 4, :], lse[:, t : t + 128], mean[:, t : t + 128]] + own
            out_ref[z * NX + owner, 8:16, :] = jnp.concatenate(rows, axis=0)


def weights(logs, means):
    peak = jnp.max(logs, axis=0, keepdims=True)
    e = jnp.exp(logs - peak)
    total = jnp.sum(e, axis=0, keepdims=True)
    w = e / total
    offset = jnp.sum(w * means, axis=0, keepdims=True)
    return peak + jnp.log(total), offset, w


def three(a):
    first = a.astype(BF16).astype(F32)
    second = (a - first).astype(BF16).astype(F32)
    return [first, second, a - first - second]


def add_query(at_ref, in_ref, out_ref, col_ref):
    z, x = at_ref[0], at_ref[1]
    odd = lax.rem(z, 2) == 1
    low = low_lanes((8, 128))
    top = lax.broadcasted_iota(jnp.int32, (8, 128), 0) < 4
    full, half = [], []
    for u in range(NX):
        logs = jnp.concatenate([in_ref[d * NX + u, 14:15, :] for d in range(NZ)], axis=0)
        means = jnp.concatenate([in_ref[d * NX + u, 15:16, :] for d in range(NZ)], axis=0)
        _, offset, w = weights(logs, means)
        shift = w * (means - offset)
        col_ref[u] = jnp.concatenate([w, shift, jnp.zeros((112, 128), F32)], axis=0).T
        cols = col_ref[u, pl.ds(pl.multiple_of(8 * z, 8), 8), :]
        ends = col_ref[u, pl.ds(pl.multiple_of(64 + 8 * (z // 2), 8), 8), :]
        ends = jnp.where(odd, pltpu.roll(ends, 4, 0), ends)
        a = jnp.zeros((8, 128), F32)
        b = jnp.zeros((8, 128), F32)
        for d in range(NZ):
            tile = in_ref[d * NX + u]
            a += tile[0:8] * jnp.where(low, cols[:, d : d + 1], cols[:, 8 + d : 9 + d])
            b += tile[8:16] * jnp.where(low, ends[:, d : d + 1], ends[:, 8 + d : 9 + d])
        full.append(a + pltpu.roll(a, 64, 1))
        half.append(b + pltpu.roll(b, 64, 1))
    f = [jnp.where(low, full[2 * p], full[2 * p + 1]) for p in range(2)]
    h = [jnp.where(low, half[2 * p], half[2 * p + 1]) for p in range(2)]
    logs = jnp.concatenate([in_ref[d * NX + x, 12:13, :] for d in range(NZ)], axis=0)
    means = jnp.concatenate([in_ref[d * NX + x, 13:14, :] for d in range(NZ)], axis=0)
    lse, offset, _ = weights(logs, means)
    stats = three(lse) + three(offset) + [jnp.zeros((2, 128), F32)]
    piece = jnp.concatenate([f[0], f[1], jnp.where(top, h[0], pltpu.roll(h[1], 4, 0))] + stats, axis=0)
    out_ref[...] = jnp.broadcast_to(piece.astype(BF16)[None], out_ref.shape)


def by_core(at_ref, a, b):
    first = at_ref[0] == 0
    return jnp.where(first, a, b), jnp.where(first, b, a)


def join_query(at_ref, own_ref, other_ref, out_ref):
    low = low_lanes((8, 128))
    top = lax.broadcasted_iota(jnp.int32, (8, 128), 0) < 4
    for y in range(NY):

        def heads(f0, f1):
            return jnp.where(low, f0, pltpu.roll(f1, 64, 1)), jnp.where(low, pltpu.roll(f0, 64, 1), f1)

        for z4 in range(0, NZ, 4):
            where = [(z4 + i) * NY + y for i in range(4)]
            pairs = [by_core(at_ref, own_ref[w].astype(F32), other_ref[w].astype(F32)) for w in where]
            pieces = [[pairs[i][c] for i in range(4)] for c in range(NC)]
            for p in range(2):
                tiles = [heads(pieces[0][i][8 * p : 8 * p + 8], pieces[1][i][8 * p : 8 * p + 8]) for i in range(4)]
                ends = []
                for i in (0, 2):
                    g = []
                    for c in range(NC):
                        even, odd = pieces[c][i][16:24], pieces[c][i + 1][16:24]
                        if p == 0:
                            g.append(jnp.where(top, even, pltpu.roll(odd, 4, 0)))
                        else:
                            g.append(jnp.where(top, pltpu.roll(even, 4, 0), odd))
                    ends.append(heads(g[0], g[1]))
                for u in range(2):
                    lanes = slice(((2 * p + u) * NY + y) * 128, ((2 * p + u) * NY + y) * 128 + 128)
                    for i in (0, 2):
                        r = 8 * (z4 + i)
                        both = jnp.concatenate([tiles[i][u], tiles[i + 1][u]], axis=0)
                        out_ref[r : r + 16, lanes] = both.astype(BF16)
                    r = 64 + 4 * z4
                    both = jnp.concatenate([ends[0][u], ends[1][u]], axis=0)
                    out_ref[r : r + 16, lanes] = both.astype(BF16)


def head_grads(told_ref, y, kv, qs):
    logs, offsets = [], []
    for t in range(3):
        piece = told_ref[t * NY + y].astype(F32)
        logs.append(piece[24:25] + piece[25:26] + piece[26:27])
        offsets.append(piece[27:28] + piece[28:29] + piece[29:30])
    lse = jnp.concatenate(logs, axis=1)
    offset = jnp.concatenate(offsets, axis=1)
    q, g = halves(jnp.concatenate([q_ref[y] for q_ref in qs], axis=0))
    prob = jnp.exp(dot(kv, q, NT) - lse)
    ds = (prob * (dot(kv, g, NT) - offset)).astype(BF16)
    return dot(ds, q, NN) + dot(prob.astype(BF16), g, NN)


def chip_grads(told_ref, own_ref, away_ref, q0, q1, q2, q3, mine_ref, sent_ref):
    for y in range(NY):
        kv = jnp.concatenate([own_ref[y], away_ref[y]], axis=0)
        out = head_grads(told_ref, y, kv, (q0, q1, q2, q3)).astype(BF16)
        mine_ref[y] = out[:BLOCK]
        sent_ref[y] = out[BLOCK:]


def join_memory(core_ref, own_ref, other_ref, k_ref, v_ref):
    low = low_lanes((BLOCK, 128))
    for y in range(NY):
        a, b = by_core(core_ref, own_ref[y].astype(F32), other_ref[y].astype(F32))
        lanes = slice(128 * y, 128 * y + 128)
        k_ref[:, lanes] = jnp.where(low, a, pltpu.roll(b, 64, 1)).astype(BF16)
        v_ref[:, lanes] = jnp.where(low, pltpu.roll(a, 64, 1), b).astype(BF16)


def around(parts):
    return parts[:1] + [
        lax.ppermute(parts[k], "row", [(i, (i + k) % NX) for i in range(NX)]) for k in range(1, NX)
    ]


def local(query, out_grad, keys, values):
    shape = jax.ShapeDtypeStruct
    z, y, c = lax.axis_index("z"), lax.axis_index("y"), lax.axis_index("core")
    x = lax.axis_index("row")
    at = jnp.stack([x, y, c]).astype(jnp.int32)
    zx = jnp.stack([z, x]).astype(jnp.int32)
    corez = c.astype(jnp.int32)[None]
    mega = 2**20

    half = shape((NY, BLOCK, 128), BF16)
    home, home_own, home_away = fetching(
        pack_memory,
        [shape((HEADS, BLOCK, 128), BF16), half, half],
        2,
        [pltpu.VMEM((BLOCK, 1024), BF16)] * 2 + [pltpu.SemaphoreType.DMA((2, 2))],
    )(corez, keys, values)
    memory = lax.all_to_all(home, ("y", "core"), 0, 0, tiled=True).reshape(MEMS, 128)
    mine = call(pack_mine, [shape((MINE, 128), BF16)] * NX, 2, smem=1, moved=mega)(at, query, out_grad)
    mine = around(list(mine))
    away = lax.ppermute(home_away, "core", SWAP)

    work = 2 * MEMS * ROWS * 128
    part = call(
        local_part,
        shape((NZ * NX, 16, 128), F32),
        5,
        smem=1,
        scratch=[pltpu.VMEM((MEMS, ROWS), F32)] * 2 + [pltpu.VMEM((MEMS, ROWS), BF16)] * 2,
        flops=4 * work,
        moved=mega,
        exps=MEMS * ROWS,
    )(at, memory, *mine)
    part = lax.all_to_all(part, ("z", "row"), 0, 0, tiled=True)
    heads = call(pack_query, [shape((NY, MINE, 128), BF16)] * NX, 2, smem=1, moved=3 * mega)(at, query, out_grad)
    part, away, *heads = lax.optimization_barrier((part, away, *heads))
    piece = call(
        add_query,
        shape((NZ * NY, 32, 128), BF16),
        1,
        smem=1,
        scratch=[pltpu.VMEM((NX, 128, 128), F32)],
        moved=mega,
    )(zx, part)
    piece = lax.all_to_all(piece, ("z", "y"), 0, 0, tiled=True)
    heads = around(list(heads))
    piece, *heads = lax.optimization_barrier((piece, *heads))
    other = lax.ppermute(piece, "core", SWAP)
    grads, sent = call(chip_grads, [half, half], 7, flops=4 * work, moved=2 * mega, exps=MEMS * ROWS)(
        piece, home_own, away, *heads
    )
    sent = lax.ppermute(sent, "core", SWAP)
    query_grad = call(join_query, shape((MINE, 4096), BF16), 2, smem=1, moved=2 * mega)(corez, piece, other)
    sent, query_grad = lax.optimization_barrier((sent, query_grad))
    key_grad, value_grad = call(join_memory, [shape((BLOCK, 1024), BF16)] * 2, 2, smem=1, moved=mega)(
        corez, grads, sent
    )
    return (query_grad, key_grad, value_grad)


def solution(mesh):
    fine = Mesh(mesh.devices.reshape(NZ, NY, NC, NX), ("z", "y", "core", "row"))
    psg = ("z", "y", "core")
    placed = (P("row", None), P("row", None), P(psg, "row"), P(psg, "row"))
    return jax.shard_map(
        local,
        mesh=fine,
        in_specs=placed,
        out_specs=(P("row", None), P(psg, "row"), P(psg, "row")),
        check_vma=False,
    )
```

```python
import jax
import jax.numpy as jnp
from jax import lax
from jax.experimental import pallas as pl
from jax.experimental.pallas import tpu as pltpu
from jax.sharding import Mesh
from jax.sharding import PartitionSpec as P

F32 = jnp.float32
BF16 = jnp.bfloat16
NZ, NY, NC, NX = 8, 8, 2, 4
HEADS = 16
BLOCK = 128
ROWS = 384
MINE = ROWS // NX
MEMS = HEADS * BLOCK
STEP = 256
NT = (((1,), (1,)), ((), ()))
TN = (((0,), (0,)), ((), ()))
SWAP = [(0, 1), (1, 0)]
NN = (((1,), (0,)), ((), ()))

VMEM = pl.BlockSpec(memory_space=pltpu.VMEM)
SMEM = pl.BlockSpec(memory_space=pltpu.SMEM)


def call(body, out_shape, n_in, scratch=(), smem=0, flops=0, moved=0, exps=0):
    outs = out_shape if isinstance(out_shape, (tuple, list)) else None
    return pl.pallas_call(
        body,
        out_shape=out_shape,
        in_specs=[SMEM] * smem + [VMEM] * n_in,
        out_specs=[VMEM] * len(outs) if outs else VMEM,
        scratch_shapes=list(scratch),
        compiler_params=pltpu.CompilerParams(vmem_limit_bytes=24 * 2**20),
        cost_estimate=pl.CostEstimate(flops=flops, bytes_accessed=moved, transcendentals=exps),
    )


def dot(a, b, dims):
    return lax.dot_general(a, b, dims, preferred_element_type=F32)


def low_lanes(shape):
    return lax.broadcasted_iota(jnp.int32, shape, len(shape) - 1) < 64


def pack_memory(k_hbm, v_hbm, out_ref, k_ref, v_ref, sems):
    copies = []
    for i in range(2):
        lanes = pl.ds(512 * i, 512)
        copies.append(pltpu.make_async_copy(k_hbm.at[:, lanes], k_ref.at[:, lanes], sems.at[0, i]))
        copies.append(pltpu.make_async_copy(v_hbm.at[:, lanes], v_ref.at[:, lanes], sems.at[1, i]))
    for copy in copies:
        copy.start()
    for t in range(HEADS // 2):
        if t % 4 == 0:
            copies[t // 2].wait()
            copies[t // 2 + 1].wait()
        k = k_ref[:, 128 * t : 128 * t + 128]
        v = v_ref[:, 128 * t : 128 * t + 128]
        out_ref[2 * t] = jnp.concatenate([k[:, :64], v[:, :64]], axis=1)
        out_ref[2 * t + 1] = jnp.concatenate([k[:, 64:], v[:, 64:]], axis=1)


def split_heads(core_ref, in_ref, own_ref, away_ref):
    c = core_ref[0]
    for t in range(HEADS // 2):
        own_ref[t] = in_ref[2 * t + c]
        away_ref[t] = in_ref[2 * t + 1 - c]


def pack_mine(at_ref, q_ref, g_ref, *outs):
    x, y, c = at_ref[0], at_ref[1], at_ref[2]
    low = low_lanes((MINE, 128))
    for k in range(NX):
        lanes = pl.ds(pl.multiple_of((lax.rem(x + k, NX) * NY + y) * 128, 128), 128)
        q = q_ref[:, lanes].astype(F32)
        g = g_ref[:, lanes].astype(F32)
        first = jnp.where(low, q, pltpu.roll(g, 64, 1))
        second = jnp.where(low, pltpu.roll(q, 64, 1), g)
        outs[k][...] = jnp.where(c == 0, first, second).astype(BF16)


def pack_query(at_ref, q_ref, g_ref, *outs):
    x, c = at_ref[0], at_ref[2]
    low = low_lanes((MINE, 128))
    for k in range(NX):
        start = lax.rem(x + k, NX) * 1024
        for t in range(HEADS // 2):
            lanes = pl.ds(pl.multiple_of(start + 128 * t, 128), 128)
            q = q_ref[:, lanes].astype(F32)
            g = g_ref[:, lanes].astype(F32)
            first = jnp.where(low, q, pltpu.roll(g, 64, 1))
            second = jnp.where(low, pltpu.roll(q, 64, 1), g)
            outs[k][t] = jnp.where(c == 0, first, second).astype(BF16)


def halves(qg):
    low = low_lanes(qg.shape)
    zero = jnp.zeros_like(qg)
    return jnp.where(low, qg, zero), jnp.where(low, zero, qg)


def local_part(at_ref, kv_ref, q0, q1, q2, q3, out_ref, s_ref, gp_ref, terms_ref):
    x = at_ref[0]
    q, g = halves(jnp.concatenate([q0[...], q1[...], q2[...], q3[...]], axis=0))
    kv = kv_ref[...]
    for r in range(0, ROWS, 128):
        rows = slice(r, r + 128)
        s_ref[rows, :] = dot(q[rows], kv, NT)
        gp_ref[rows, :] = dot(g[rows], kv, NT)
    blocks = [slice(j, j + 128) for j in range(0, MEMS, 128)]
    lses, means = [], []
    for r in range(0, ROWS, 128):
        rows = slice(r, r + 128)
        top = s_ref[rows, blocks[0]]
        for j in blocks[1:]:
            top = jnp.maximum(top, s_ref[rows, j])
        peak = jnp.max(top, axis=1, keepdims=True)
        total = jnp.zeros((128, 128), F32)
        weighted = jnp.zeros((128, 128), F32)
        for j in blocks:
            e = jnp.exp(s_ref[rows, j] - peak)
            s_ref[rows, j] = e
            total += e
            weighted += e * gp_ref[rows, j]
        total = jnp.sum(total, axis=1, keepdims=True)
        inverse = 1.0 / total
        mean = jnp.sum(weighted, axis=1, keepdims=True) * inverse
        lses.append(peak + jnp.log(total))
        means.append(mean)
        for j in blocks:
            prob = s_ref[rows, j] * inverse
            terms_ref[rows, j] = (prob * (gp_ref[rows, j] - mean)).astype(BF16)
            terms_ref[ROWS + r : ROWS + r + 128, j] = prob.astype(BF16)
    both = dot(terms_ref[...], kv, NN)
    both = jnp.where(low_lanes((ROWS, 128)), both[:ROWS], pltpu.roll(both[ROWS:], 64, 1))
    first = lax.broadcasted_iota(jnp.int32, (128, 128), 1) == 0
    turned = [jnp.where(first, a, b).T for a, b in zip(lses, means)]
    lse = jnp.concatenate([a[0:1] for a in turned], axis=1)
    mean = jnp.concatenate([a[1:2] for a in turned], axis=1)
    pad = jnp.zeros((1, 128 - MINE), F32)
    for r in range(NX):
        owner = lax.rem(x - r + NX, NX)
        own = [jnp.concatenate([a[:, MINE * r : MINE * r + MINE], pad], axis=1) for a in (lse, mean)]
        for z in range(NZ):
            t = 128 * min(z, 2)
            a = MINE * r + 8 * z
            b = MINE * r + 64 + 4 * z
            out_ref[z * NX + owner, 0:8, :] = both[a : a + 8, :]
            rows = [both[b : b + 4, :], lse[:, t : t + 128], mean[:, t : t + 128]] + own
            out_ref[z * NX + owner, 8:16, :] = jnp.concatenate(rows, axis=0)


def weights(logs, means):
    peak = jnp.max(logs, axis=0, keepdims=True)
    e = jnp.exp(logs - peak)
    total = jnp.sum(e, axis=0, keepdims=True)
    w = e / total
    offset = jnp.sum(w * means, axis=0, keepdims=True)
    return peak + jnp.log(total), offset, w


def three(a):
    first = a.astype(BF16).astype(F32)
    second = (a - first).astype(BF16).astype(F32)
    return [first, second, a - first - second]


def add_query(at_ref, in_ref, out_ref, col_ref):
    z, x = at_ref[0], at_ref[1]
    odd = lax.rem(z, 2) == 1
    low = low_lanes((8, 128))
    top = lax.broadcasted_iota(jnp.int32, (8, 128), 0) < 4
    full, half = [], []
    for u in range(NX):
        logs = jnp.concatenate([in_ref[d * NX + u, 14:15, :] for d in range(NZ)], axis=0)
        means = jnp.concatenate([in_ref[d * NX + u, 15:16, :] for d in range(NZ)], axis=0)
        _, offset, w = weights(logs, means)
        shift = w * (means - offset)
        col_ref[u] = jnp.concatenate([w, shift, jnp.zeros((112, 128), F32)], axis=0).T
        cols = col_ref[u, pl.ds(pl.multiple_of(8 * z, 8), 8), :]
        ends = col_ref[u, pl.ds(pl.multiple_of(64 + 8 * (z // 2), 8), 8), :]
        ends = jnp.where(odd, pltpu.roll(ends, 4, 0), ends)
        a = jnp.zeros((8, 128), F32)
        b = jnp.zeros((8, 128), F32)
        for d in range(NZ):
            tile = in_ref[d * NX + u]
            a += tile[0:8] * jnp.where(low, cols[:, d : d + 1], cols[:, 8 + d : 9 + d])
            b += tile[8:16] * jnp.where(low, ends[:, d : d + 1], ends[:, 8 + d : 9 + d])
        full.append(a + pltpu.roll(a, 64, 1))
        half.append(b + pltpu.roll(b, 64, 1))
    f = [jnp.where(low, full[2 * p], full[2 * p + 1]) for p in range(2)]
    h = [jnp.where(low, half[2 * p], half[2 * p + 1]) for p in range(2)]
    logs = jnp.concatenate([in_ref[d * NX + x, 12:13, :] for d in range(NZ)], axis=0)
    means = jnp.concatenate([in_ref[d * NX + x, 13:14, :] for d in range(NZ)], axis=0)
    lse, offset, _ = weights(logs, means)
    stats = three(lse) + three(offset) + [jnp.zeros((2, 128), F32)]
    piece = jnp.concatenate([f[0], f[1], jnp.where(top, h[0], pltpu.roll(h[1], 4, 0))] + stats, axis=0)
    out_ref[...] = jnp.broadcast_to(piece.astype(BF16)[None], out_ref.shape)


def by_core(at_ref, a, b):
    first = at_ref[0] == 0
    return jnp.where(first, a, b), jnp.where(first, b, a)


def join_rows(at_ref, own_ref, other_ref, out_ref, y, z4):
    low = low_lanes((8, 128))
    top = lax.broadcasted_iota(jnp.int32, (8, 128), 0) < 4

    def heads(f0, f1):
        return jnp.where(low, f0, pltpu.roll(f1, 64, 1)), jnp.where(low, pltpu.roll(f0, 64, 1), f1)

    where = [(z4 + i) * NY + y for i in range(4)]
    pairs = [by_core(at_ref, own_ref[w].astype(F32), other_ref[w].astype(F32)) for w in where]
    pieces = [[pairs[i][c] for i in range(4)] for c in range(NC)]
    for p in range(2):
        tiles = [heads(pieces[0][i][8 * p : 8 * p + 8], pieces[1][i][8 * p : 8 * p + 8]) for i in range(4)]
        ends = []
        for i in (0, 2):
            g = []
            for c in range(NC):
                even, odd = pieces[c][i][16:24], pieces[c][i + 1][16:24]
                if p == 0:
                    g.append(jnp.where(top, even, pltpu.roll(odd, 4, 0)))
                else:
                    g.append(jnp.where(top, pltpu.roll(even, 4, 0), odd))
            ends.append(heads(g[0], g[1]))
        for u in range(2):
            lanes = slice(((2 * p + u) * NY + y) * 128, ((2 * p + u) * NY + y) * 128 + 128)
            for i in (0, 2):
                r = 8 * (z4 + i)
                both = jnp.concatenate([tiles[i][u], tiles[i + 1][u]], axis=0)
                out_ref[r : r + 16, lanes] = both.astype(BF16)
            r = 64 + 4 * z4
            both = jnp.concatenate([ends[0][u], ends[1][u]], axis=0)
            out_ref[r : r + 16, lanes] = both.astype(BF16)


def sender(sems):
    copies = []

    def send(src, dst):
        copy = pltpu.make_async_copy(src, dst, sems.at[len(copies)])
        copy.start()
        copies.append(copy)

    return copies, send


def join_query(at_ref, own_ref, other_ref, q_hbm, q_ref, sems):
    copies, send = sender(sems)
    for z4 in range(0, NZ, 4):
        for y in range(NY):
            join_rows(at_ref, own_ref, other_ref, q_ref, y, z4)
        for start, size in ((8 * z4, 32), (64 + 4 * z4, 16)):
            rows = pl.ds(start, size)
            send(q_ref.at[rows, :], q_hbm.at[rows, :])
    for copy in copies:
        copy.wait()


def join_memory(at_ref, grads_ref, sent_ref, k_hbm, v_hbm, k_ref, v_ref, sems):
    copies, send = sender(sems)
    low = low_lanes((BLOCK, 128))
    for y in range(NY):
        a, b = by_core(at_ref, grads_ref[y].astype(F32), sent_ref[y].astype(F32))
        lanes = slice(128 * y, 128 * y + 128)
        k_ref[:, lanes] = jnp.where(low, a, pltpu.roll(b, 64, 1)).astype(BF16)
        v_ref[:, lanes] = jnp.where(low, pltpu.roll(a, 64, 1), b).astype(BF16)
        if y % 2 == 1:
            part = pl.ds(128 * (y - 1), 256)
            send(k_ref.at[:, part], k_hbm.at[:, part])
            send(v_ref.at[:, part], v_hbm.at[:, part])
    for copy in copies:
        copy.wait()


def head_grads(told_ref, y, kv, qs):
    logs, offsets = [], []
    for t in range(3):
        piece = told_ref[t * NY + y].astype(F32)
        logs.append(piece[24:25] + piece[25:26] + piece[26:27])
        offsets.append(piece[27:28] + piece[28:29] + piece[29:30])
    lse = jnp.concatenate(logs, axis=1)
    offset = jnp.concatenate(offsets, axis=1)
    q, g = halves(jnp.concatenate([q_ref[y] for q_ref in qs], axis=0))
    prob = jnp.exp(dot(kv, q, NT) - lse)
    ds = (prob * (dot(kv, g, NT) - offset)).astype(BF16)
    return dot(ds, q, NN) + dot(prob.astype(BF16), g, NN)


def chip_grads(told_ref, own_ref, away_ref, q0, q1, q2, q3, mine_ref, sent_ref):
    for y in range(NY):
        kv = jnp.concatenate([own_ref[y], away_ref[y]], axis=0)
        out = head_grads(told_ref, y, kv, (q0, q1, q2, q3)).astype(BF16)
        mine_ref[y] = out[:BLOCK]
        sent_ref[y] = out[BLOCK:]


def around(parts):
    return parts[:1] + [
        lax.ppermute(parts[k], "row", [(i, (i + k) % NX) for i in range(NX)]) for k in range(1, NX)
    ]


def local(query, out_grad, keys, values):
    shape = jax.ShapeDtypeStruct
    z, y, c = lax.axis_index("z"), lax.axis_index("y"), lax.axis_index("core")
    x = lax.axis_index("row")
    at = jnp.stack([x, y, c]).astype(jnp.int32)
    zx = jnp.stack([z, x]).astype(jnp.int32)
    corez = c.astype(jnp.int32)[None]
    mega = 2**20

    half = shape((NY, BLOCK, 128), BF16)
    home = pl.pallas_call(
        pack_memory,
        out_shape=shape((HEADS, BLOCK, 128), BF16),
        in_specs=[pl.BlockSpec(memory_space=pl.ANY)] * 2,
        out_specs=VMEM,
        scratch_shapes=[pltpu.VMEM((BLOCK, 1024), BF16)] * 2 + [pltpu.SemaphoreType.DMA((2, 2))],
        compiler_params=pltpu.CompilerParams(vmem_limit_bytes=60 * 2**20),
        cost_estimate=pl.CostEstimate(flops=0, bytes_accessed=mega, transcendentals=0),
    )(keys, values)
    memory = lax.all_to_all(home, ("y", "core"), 0, 0, tiled=True).reshape(MEMS, 128)
    mine = call(pack_mine, [shape((MINE, 128), BF16)] * NX, 2, smem=1, moved=mega)(at, query, out_grad)
    mine = around(list(mine))
    home_own, home_away = call(split_heads, [half, half], 1, smem=1, moved=mega)(corez, home)
    away = lax.ppermute(home_away, "core", SWAP)

    work = 2 * MEMS * ROWS * 128
    part = call(
        local_part,
        shape((NZ * NX, 16, 128), F32),
        5,
        smem=1,
        scratch=[pltpu.VMEM((ROWS, MEMS), F32)] * 2 + [pltpu.VMEM((2 * ROWS, MEMS), BF16)],
        flops=4 * work,
        moved=mega,
        exps=MEMS * ROWS,
    )(at, memory, *mine)
    part = lax.all_to_all(part, ("z", "row"), 0, 0, tiled=True)
    heads = call(pack_query, [shape((NY, MINE, 128), BF16)] * NX, 2, smem=1, moved=3 * mega)(at, query, out_grad)
    part, away, *heads = lax.optimization_barrier((part, away, *heads))
    piece = call(
        add_query,
        shape((NZ * NY, 32, 128), BF16),
        1,
        smem=1,
        scratch=[pltpu.VMEM((NX, 128, 128), F32)],
        moved=mega,
    )(zx, part)
    piece = lax.all_to_all(piece, ("z", "y"), 0, 0, tiled=True)
    heads = around(list(heads))
    piece, *heads = lax.optimization_barrier((piece, *heads))
    other = lax.ppermute(piece, "core", SWAP)
    grads, sent = call(chip_grads, [half, half], 7, flops=4 * work, moved=2 * mega, exps=MEMS * ROWS)(
        piece, home_own, away, *heads
    )
    sent = lax.ppermute(sent, "core", SWAP)
    def joined(body, results, count):
        return pl.pallas_call(
            body,
            out_shape=results,
            in_specs=[SMEM] + [VMEM] * 2,
            out_specs=[pl.BlockSpec(memory_space=pl.ANY)] * len(results),
            scratch_shapes=[pltpu.VMEM(a.shape, a.dtype) for a in results] + [pltpu.SemaphoreType.DMA((count,))],
            compiler_params=pltpu.CompilerParams(vmem_limit_bytes=24 * 2**20),
            cost_estimate=pl.CostEstimate(flops=0, bytes_accessed=2 * mega, transcendentals=0),
        )

    (query_grad,) = joined(join_query, [shape((MINE, 4096), BF16)], 4)(corez, piece, other)
    sent, query_grad = lax.optimization_barrier((sent, query_grad))
    key_grad, value_grad = joined(join_memory, [shape((BLOCK, 1024), BF16)] * 2, 8)(corez, grads, sent)
    return (query_grad, key_grad, value_grad)


def solution(mesh):
    fine = Mesh(mesh.devices.reshape(NZ, NY, NC, NX), ("z", "y", "core", "row"))
    psg = ("z", "y", "core")
    placed = (P("row", None), P("row", None), P(psg, "row"), P(psg, "row"))
    return jax.shard_map(
        local,
        mesh=fine,
        in_specs=placed,
        out_specs=(P("row", None), P(psg, "row"), P(psg, "row")),
        check_vma=False,
    )
```

```python
import jax
import jax.numpy as jnp
from jax import lax
from jax.experimental import pallas as pl
from jax.experimental.pallas import tpu as pltpu
from jax.sharding import Mesh
from jax.sharding import PartitionSpec as P

F32 = jnp.float32
BF16 = jnp.bfloat16
NZ, NY, NC, NX = 8, 8, 2, 4
HEADS = 16
BLOCK = 128
ROWS = 384
MINE = ROWS // NX
MEMS = HEADS * BLOCK
STEP = 256
NT = (((1,), (1,)), ((), ()))
TN = (((0,), (0,)), ((), ()))
SWAP = [(0, 1), (1, 0)]
NN = (((1,), (0,)), ((), ()))

VMEM = pl.BlockSpec(memory_space=pltpu.VMEM)
SMEM = pl.BlockSpec(memory_space=pltpu.SMEM)


def call(body, out_shape, n_in, scratch=(), smem=0, flops=0, moved=0, exps=0):
    outs = out_shape if isinstance(out_shape, (tuple, list)) else None
    return pl.pallas_call(
        body,
        out_shape=out_shape,
        in_specs=[SMEM] * smem + [VMEM] * n_in,
        out_specs=[VMEM] * len(outs) if outs else VMEM,
        scratch_shapes=list(scratch),
        compiler_params=pltpu.CompilerParams(vmem_limit_bytes=24 * 2**20),
        cost_estimate=pl.CostEstimate(flops=flops, bytes_accessed=moved, transcendentals=exps),
    )


def dot(a, b, dims):
    return lax.dot_general(a, b, dims, preferred_element_type=F32)


def low_lanes(shape):
    return lax.broadcasted_iota(jnp.int32, shape, len(shape) - 1) < 64


def pack_memory(k_hbm, v_hbm, out_ref, k_ref, v_ref, sems):
    copies = []
    for i in range(2):
        lanes = pl.ds(512 * i, 512)
        copies.append(pltpu.make_async_copy(k_hbm.at[:, lanes], k_ref.at[:, lanes], sems.at[0, i]))
        copies.append(pltpu.make_async_copy(v_hbm.at[:, lanes], v_ref.at[:, lanes], sems.at[1, i]))
    for copy in copies:
        copy.start()
    for t in range(HEADS // 2):
        if t % 4 == 0:
            copies[t // 2].wait()
            copies[t // 2 + 1].wait()
        k = k_ref[:, 128 * t : 128 * t + 128]
        v = v_ref[:, 128 * t : 128 * t + 128]
        out_ref[2 * t] = jnp.concatenate([k[:, :64], v[:, :64]], axis=1)
        out_ref[2 * t + 1] = jnp.concatenate([k[:, 64:], v[:, 64:]], axis=1)


def split_heads(core_ref, in_ref, own_ref, away_ref):
    c = core_ref[0]
    for t in range(HEADS // 2):
        own_ref[t] = in_ref[2 * t + c]
        away_ref[t] = in_ref[2 * t + 1 - c]


def pack_mine(at_ref, q_ref, g_ref, *outs):
    x, y, c = at_ref[0], at_ref[1], at_ref[2]
    low = low_lanes((MINE, 128))
    for k in range(NX):
        lanes = pl.ds(pl.multiple_of((lax.rem(x + k, NX) * NY + y) * 128, 128), 128)
        q = q_ref[:, lanes].astype(F32)
        g = g_ref[:, lanes].astype(F32)
        first = jnp.where(low, q, pltpu.roll(g, 64, 1))
        second = jnp.where(low, pltpu.roll(q, 64, 1), g)
        outs[k][...] = jnp.where(c == 0, first, second).astype(BF16)


def pack_query(at_ref, q_ref, g_ref, *outs):
    x, c = at_ref[0], at_ref[2]
    low = low_lanes((MINE, 128))
    for k in range(NX):
        start = lax.rem(x + k, NX) * 1024
        for t in range(HEADS // 2):
            lanes = pl.ds(pl.multiple_of(start + 128 * t, 128), 128)
            q = q_ref[:, lanes].astype(F32)
            g = g_ref[:, lanes].astype(F32)
            first = jnp.where(low, q, pltpu.roll(g, 64, 1))
            second = jnp.where(low, pltpu.roll(q, 64, 1), g)
            outs[k][t] = jnp.where(c == 0, first, second).astype(BF16)


def halves(qg):
    low = low_lanes(qg.shape)
    zero = jnp.zeros_like(qg)
    return jnp.where(low, qg, zero), jnp.where(low, zero, qg)


def local_part(at_ref, kv_ref, q0, q1, q2, q3, out_ref, s_ref, gp_ref, terms_ref):
    x = at_ref[0]
    q, g = halves(jnp.concatenate([q0[...], q1[...], q2[...], q3[...]], axis=0))
    kv = kv_ref[...]
    for r in range(0, ROWS, 128):
        rows = slice(r, r + 128)
        s_ref[rows, :] = dot(q[rows], kv, NT)
        gp_ref[rows, :] = dot(g[rows], kv, NT)
    blocks = [slice(j, j + 128) for j in range(0, MEMS, 128)]
    lses, means = [], []
    for r in range(0, ROWS, 128):
        rows = slice(r, r + 128)
        top = s_ref[rows, blocks[0]]
        for j in blocks[1:]:
            top = jnp.maximum(top, s_ref[rows, j])
        peak = jnp.max(top, axis=1, keepdims=True)
        total = jnp.zeros((128, 128), F32)
        weighted = jnp.zeros((128, 128), F32)
        for j in blocks:
            e = jnp.exp(s_ref[rows, j] - peak)
            s_ref[rows, j] = e
            total += e
            weighted += e * gp_ref[rows, j]
        total = jnp.sum(total, axis=1, keepdims=True)
        inverse = 1.0 / total
        mean = jnp.sum(weighted, axis=1, keepdims=True) * inverse
        lses.append(peak + jnp.log(total))
        means.append(mean)
        for j in blocks:
            prob = s_ref[rows, j] * inverse
            terms_ref[rows, j] = (prob * (gp_ref[rows, j] - mean)).astype(BF16)
            terms_ref[ROWS + r : ROWS + r + 128, j] = prob.astype(BF16)
    both = dot(terms_ref[...], kv, NN)
    both = jnp.where(low_lanes((ROWS, 128)), both[:ROWS], pltpu.roll(both[ROWS:], 64, 1))
    first = lax.broadcasted_iota(jnp.int32, (128, 128), 1) == 0
    turned = [jnp.where(first, a, b).T for a, b in zip(lses, means)]
    lse = jnp.concatenate([a[0:1] for a in turned], axis=1)
    mean = jnp.concatenate([a[1:2] for a in turned], axis=1)
    pad = jnp.zeros((1, 128 - MINE), F32)
    for r in range(NX):
        owner = lax.rem(x - r + NX, NX)
        own = [jnp.concatenate([a[:, MINE * r : MINE * r + MINE], pad], axis=1) for a in (lse, mean)]
        for z in range(NZ):
            t = 128 * min(z, 2)
            a = MINE * r + 8 * z
            b = MINE * r + 64 + 4 * z
            out_ref[owner * NZ + z, 0:8, :] = both[a : a + 8, :]
            rows = [both[b : b + 4, :], lse[:, t : t + 128], mean[:, t : t + 128]] + own
            out_ref[owner * NZ + z, 8:16, :] = jnp.concatenate(rows, axis=0)


def weights(logs, means):
    peak = jnp.max(logs, axis=0, keepdims=True)
    e = jnp.exp(logs - peak)
    total = jnp.sum(e, axis=0, keepdims=True)
    w = e / total
    offset = jnp.sum(w * means, axis=0, keepdims=True)
    return peak + jnp.log(total), offset, w


def three(a):
    first = a.astype(BF16).astype(F32)
    second = (a - first).astype(BF16).astype(F32)
    return [first, second, a - first - second]


def add_query(at_ref, in_ref, out_ref, col_ref):
    z, x = at_ref[0], at_ref[1]
    odd = lax.rem(z, 2) == 1
    low = low_lanes((8, 128))
    top = lax.broadcasted_iota(jnp.int32, (8, 128), 0) < 4
    full, half = [], []
    for u in range(NX):
        logs = jnp.concatenate([in_ref[u * NZ + d, 14:15, :] for d in range(NZ)], axis=0)
        means = jnp.concatenate([in_ref[u * NZ + d, 15:16, :] for d in range(NZ)], axis=0)
        _, offset, w = weights(logs, means)
        shift = w * (means - offset)
        col_ref[u] = jnp.concatenate([w, shift, jnp.zeros((112, 128), F32)], axis=0).T
        cols = col_ref[u, pl.ds(pl.multiple_of(8 * z, 8), 8), :]
        ends = col_ref[u, pl.ds(pl.multiple_of(64 + 8 * (z // 2), 8), 8), :]
        ends = jnp.where(odd, pltpu.roll(ends, 4, 0), ends)
        a = jnp.zeros((8, 128), F32)
        b = jnp.zeros((8, 128), F32)
        for d in range(NZ):
            tile = in_ref[u * NZ + d]
            a += tile[0:8] * jnp.where(low, cols[:, d : d + 1], cols[:, 8 + d : 9 + d])
            b += tile[8:16] * jnp.where(low, ends[:, d : d + 1], ends[:, 8 + d : 9 + d])
        full.append(a + pltpu.roll(a, 64, 1))
        half.append(b + pltpu.roll(b, 64, 1))
    f = [jnp.where(low, full[2 * p], full[2 * p + 1]) for p in range(2)]
    h = [jnp.where(low, half[2 * p], half[2 * p + 1]) for p in range(2)]
    logs = jnp.concatenate([in_ref[x * NZ + d, 12:13, :] for d in range(NZ)], axis=0)
    means = jnp.concatenate([in_ref[x * NZ + d, 13:14, :] for d in range(NZ)], axis=0)
    lse, offset, _ = weights(logs, means)
    stats = three(lse) + three(offset) + [jnp.zeros((2, 128), F32)]
    piece = jnp.concatenate([f[0], f[1], jnp.where(top, h[0], pltpu.roll(h[1], 4, 0))] + stats, axis=0)
    out_ref[...] = jnp.broadcast_to(piece.astype(BF16)[None], out_ref.shape)


def by_core(at_ref, a, b):
    first = at_ref[0] == 0
    return jnp.where(first, a, b), jnp.where(first, b, a)


def join_rows(at_ref, own_ref, other_ref, out_ref, y, z4):
    low = low_lanes((8, 128))
    top = lax.broadcasted_iota(jnp.int32, (8, 128), 0) < 4

    def heads(f0, f1):
        return jnp.where(low, f0, pltpu.roll(f1, 64, 1)), jnp.where(low, pltpu.roll(f0, 64, 1), f1)

    where = [y * NZ + z4 + i for i in range(4)]
    pairs = [by_core(at_ref, own_ref[w].astype(F32), other_ref[w].astype(F32)) for w in where]
    pieces = [[pairs[i][c] for i in range(4)] for c in range(NC)]
    for p in range(2):
        tiles = [heads(pieces[0][i][8 * p : 8 * p + 8], pieces[1][i][8 * p : 8 * p + 8]) for i in range(4)]
        ends = []
        for i in (0, 2):
            g = []
            for c in range(NC):
                even, odd = pieces[c][i][16:24], pieces[c][i + 1][16:24]
                if p == 0:
                    g.append(jnp.where(top, even, pltpu.roll(odd, 4, 0)))
                else:
                    g.append(jnp.where(top, pltpu.roll(even, 4, 0), odd))
            ends.append(heads(g[0], g[1]))
        for u in range(2):
            lanes = slice(((2 * p + u) * NY + y) * 128, ((2 * p + u) * NY + y) * 128 + 128)
            for i in (0, 2):
                r = 8 * (z4 + i)
                both = jnp.concatenate([tiles[i][u], tiles[i + 1][u]], axis=0)
                out_ref[r : r + 16, lanes] = both.astype(BF16)
            r = 64 + 4 * z4
            both = jnp.concatenate([ends[0][u], ends[1][u]], axis=0)
            out_ref[r : r + 16, lanes] = both.astype(BF16)


def sender(sems):
    copies = []

    def send(src, dst):
        copy = pltpu.make_async_copy(src, dst, sems.at[len(copies)])
        copy.start()
        copies.append(copy)

    return copies, send


def join_query(at_ref, own_ref, other_ref, q_hbm, q_ref, sems):
    copies, send = sender(sems)
    for z4 in range(0, NZ, 4):
        for y in range(NY):
            join_rows(at_ref, own_ref, other_ref, q_ref, y, z4)
        for start, size in ((8 * z4, 32), (64 + 4 * z4, 16)):
            rows = pl.ds(start, size)
            send(q_ref.at[rows, :], q_hbm.at[rows, :])
    for copy in copies:
        copy.wait()


def join_memory(at_ref, grads_ref, sent_ref, k_hbm, v_hbm, k_ref, v_ref, sems):
    copies, send = sender(sems)
    low = low_lanes((BLOCK, 128))
    for y in range(NY):
        a, b = by_core(at_ref, grads_ref[y].astype(F32), sent_ref[y].astype(F32))
        lanes = slice(128 * y, 128 * y + 128)
        k_ref[:, lanes] = jnp.where(low, a, pltpu.roll(b, 64, 1)).astype(BF16)
        v_ref[:, lanes] = jnp.where(low, pltpu.roll(a, 64, 1), b).astype(BF16)
        if y % 2 == 1:
            part = pl.ds(128 * (y - 1), 256)
            send(k_ref.at[:, part], k_hbm.at[:, part])
            send(v_ref.at[:, part], v_hbm.at[:, part])
    for copy in copies:
        copy.wait()


def head_grads(told_ref, y, kv, qs):
    logs, offsets = [], []
    for t in range(3):
        piece = told_ref[y * NZ + t].astype(F32)
        logs.append(piece[24:25] + piece[25:26] + piece[26:27])
        offsets.append(piece[27:28] + piece[28:29] + piece[29:30])
    lse = jnp.concatenate(logs, axis=1)
    offset = jnp.concatenate(offsets, axis=1)
    q, g = halves(jnp.concatenate([q_ref[y] for q_ref in qs], axis=0))
    prob = jnp.exp(dot(kv, q, NT) - lse)
    ds = (prob * (dot(kv, g, NT) - offset)).astype(BF16)
    return dot(ds, q, NN) + dot(prob.astype(BF16), g, NN)


def chip_grads(told_ref, own_ref, away_ref, q0, q1, q2, q3, mine_ref, sent_ref):
    for y in range(NY):
        kv = jnp.concatenate([own_ref[y], away_ref[y]], axis=0)
        out = head_grads(told_ref, y, kv, (q0, q1, q2, q3)).astype(BF16)
        mine_ref[y] = out[:BLOCK]
        sent_ref[y] = out[BLOCK:]


def around(parts):
    return parts[:1] + [
        lax.ppermute(parts[k], "row", [(i, (i + k) % NX) for i in range(NX)]) for k in range(1, NX)
    ]


def local(query, out_grad, keys, values):
    shape = jax.ShapeDtypeStruct
    z, y, c = lax.axis_index("z"), lax.axis_index("y"), lax.axis_index("core")
    x = lax.axis_index("row")
    at = jnp.stack([x, y, c]).astype(jnp.int32)
    zx = jnp.stack([z, x]).astype(jnp.int32)
    corez = c.astype(jnp.int32)[None]
    mega = 2**20

    half = shape((NY, BLOCK, 128), BF16)
    home = pl.pallas_call(
        pack_memory,
        out_shape=shape((HEADS, BLOCK, 128), BF16),
        in_specs=[pl.BlockSpec(memory_space=pl.ANY)] * 2,
        out_specs=VMEM,
        scratch_shapes=[pltpu.VMEM((BLOCK, 1024), BF16)] * 2 + [pltpu.SemaphoreType.DMA((2, 2))],
        compiler_params=pltpu.CompilerParams(vmem_limit_bytes=60 * 2**20),
        cost_estimate=pl.CostEstimate(flops=0, bytes_accessed=mega, transcendentals=0),
    )(keys, values)
    memory = lax.all_to_all(home, ("y", "core"), 0, 0, tiled=True).reshape(MEMS, 128)
    mine = call(pack_mine, [shape((MINE, 128), BF16)] * NX, 2, smem=1, moved=mega)(at, query, out_grad)
    mine = around(list(mine))
    home_own, home_away = call(split_heads, [half, half], 1, smem=1, moved=mega)(corez, home)
    away = lax.ppermute(home_away, "core", SWAP)

    work = 2 * MEMS * ROWS * 128
    part = call(
        local_part,
        shape((NZ * NX, 16, 128), F32),
        5,
        smem=1,
        scratch=[pltpu.VMEM((ROWS, MEMS), F32)] * 2 + [pltpu.VMEM((2 * ROWS, MEMS), BF16)],
        flops=4 * work,
        moved=mega,
        exps=MEMS * ROWS,
    )(at, memory, *mine)
    part = lax.all_to_all(part, ("row", "z"), 0, 0, tiled=True)
    heads = call(pack_query, [shape((NY, MINE, 128), BF16)] * NX, 2, smem=1, moved=3 * mega)(at, query, out_grad)
    part, away, *heads = lax.optimization_barrier((part, away, *heads))
    piece = call(
        add_query,
        shape((NZ * NY, 32, 128), BF16),
        1,
        smem=1,
        scratch=[pltpu.VMEM((NX, 128, 128), F32)],
        moved=mega,
    )(zx, part)
    piece = lax.all_to_all(piece, ("y", "z"), 0, 0, tiled=True)
    heads = around(list(heads))
    piece, *heads = lax.optimization_barrier((piece, *heads))
    other = lax.ppermute(piece, "core", SWAP)
    grads, sent = call(chip_grads, [half, half], 7, flops=4 * work, moved=2 * mega, exps=MEMS * ROWS)(
        piece, home_own, away, *heads
    )
    sent = lax.ppermute(sent, "core", SWAP)
    def joined(body, results, count):
        return pl.pallas_call(
            body,
            out_shape=results,
            in_specs=[SMEM] + [VMEM] * 2,
            out_specs=[pl.BlockSpec(memory_space=pl.ANY)] * len(results),
            scratch_shapes=[pltpu.VMEM(a.shape, a.dtype) for a in results] + [pltpu.SemaphoreType.DMA((count,))],
            compiler_params=pltpu.CompilerParams(vmem_limit_bytes=24 * 2**20),
            cost_estimate=pl.CostEstimate(flops=0, bytes_accessed=2 * mega, transcendentals=0),
        )

    (query_grad,) = joined(join_query, [shape((MINE, 4096), BF16)], 4)(corez, piece, other)
    sent, query_grad = lax.optimization_barrier((sent, query_grad))
    key_grad, value_grad = joined(join_memory, [shape((BLOCK, 1024), BF16)] * 2, 8)(corez, grads, sent)
    return (query_grad, key_grad, value_grad)


def solution(mesh):
    fine = Mesh(mesh.devices.reshape(NZ, NY, NC, NX), ("z", "y", "core", "row"))
    psg = ("z", "y", "core")
    placed = (P("row", None), P("row", None), P(psg, "row"), P(psg, "row"))
    return jax.shard_map(
        local,
        mesh=fine,
        in_specs=placed,
        out_specs=(P("row", None), P(psg, "row"), P(psg, "row")),
        check_vma=False,
    )
```

```python
import jax
import jax.numpy as jnp
from jax import lax
from jax.experimental import pallas as pl
from jax.experimental.pallas import tpu as pltpu
from jax.sharding import Mesh
from jax.sharding import PartitionSpec as P

F32 = jnp.float32
BF16 = jnp.bfloat16
NZ, NY, NC, NX = 8, 8, 2, 4
HEADS = 16
BLOCK = 128
ROWS = 384
MINE = ROWS // NX
MEMS = HEADS * BLOCK
STEP = 256
NT = (((1,), (1,)), ((), ()))
TN = (((0,), (0,)), ((), ()))
SWAP = [(0, 1), (1, 0)]
NN = (((1,), (0,)), ((), ()))

VMEM = pl.BlockSpec(memory_space=pltpu.VMEM)
SMEM = pl.BlockSpec(memory_space=pltpu.SMEM)


def call(body, out_shape, n_in, scratch=(), smem=0, flops=0, moved=0, exps=0):
    outs = out_shape if isinstance(out_shape, (tuple, list)) else None
    return pl.pallas_call(
        body,
        out_shape=out_shape,
        in_specs=[SMEM] * smem + [VMEM] * n_in,
        out_specs=[VMEM] * len(outs) if outs else VMEM,
        scratch_shapes=list(scratch),
        compiler_params=pltpu.CompilerParams(vmem_limit_bytes=24 * 2**20),
        cost_estimate=pl.CostEstimate(flops=flops, bytes_accessed=moved, transcendentals=exps),
    )


def dot(a, b, dims):
    return lax.dot_general(a, b, dims, preferred_element_type=F32)


def low_lanes(shape):
    return lax.broadcasted_iota(jnp.int32, shape, len(shape) - 1) < 64


def pack_memory(k_hbm, v_hbm, out_ref, k_ref, v_ref, sems):
    copies = []
    for i in range(2):
        lanes = pl.ds(512 * i, 512)
        copies.append(pltpu.make_async_copy(k_hbm.at[:, lanes], k_ref.at[:, lanes], sems.at[0, i]))
        copies.append(pltpu.make_async_copy(v_hbm.at[:, lanes], v_ref.at[:, lanes], sems.at[1, i]))
    for copy in copies:
        copy.start()
    for t in range(HEADS // 2):
        if t % 4 == 0:
            copies[t // 2].wait()
            copies[t // 2 + 1].wait()
        k = k_ref[:, 128 * t : 128 * t + 128]
        v = v_ref[:, 128 * t : 128 * t + 128]
        out_ref[t] = jnp.concatenate([k[:, :64], v[:, :64]], axis=1)
        out_ref[NY + t] = jnp.concatenate([k[:, 64:], v[:, 64:]], axis=1)


def split_heads(core_ref, in_ref, own_ref, away_ref):
    c = core_ref[0]
    for t in range(HEADS // 2):
        own_ref[t] = in_ref[NY * c + t]
        away_ref[t] = in_ref[NY * (1 - c) + t]


def pack_mine(at_ref, q_ref, g_ref, *outs):
    x, y, c = at_ref[0], at_ref[1], at_ref[2]
    low = low_lanes((MINE, 128))
    for k in range(NX):
        lanes = pl.ds(pl.multiple_of((lax.rem(x + k, NX) * NY + y) * 128, 128), 128)
        q = q_ref[:, lanes].astype(F32)
        g = g_ref[:, lanes].astype(F32)
        first = jnp.where(low, q, pltpu.roll(g, 64, 1))
        second = jnp.where(low, pltpu.roll(q, 64, 1), g)
        outs[k][...] = jnp.where(c == 0, first, second).astype(BF16)


def pack_query(at_ref, q_ref, g_ref, *outs):
    x, c = at_ref[0], at_ref[2]
    low = low_lanes((MINE, 128))
    for k in range(NX):
        start = lax.rem(x + k, NX) * 1024
        for t in range(HEADS // 2):
            lanes = pl.ds(pl.multiple_of(start + 128 * t, 128), 128)
            q = q_ref[:, lanes].astype(F32)
            g = g_ref[:, lanes].astype(F32)
            first = jnp.where(low, q, pltpu.roll(g, 64, 1))
            second = jnp.where(low, pltpu.roll(q, 64, 1), g)
            outs[k][t] = jnp.where(c == 0, first, second).astype(BF16)


def halves(qg):
    low = low_lanes(qg.shape)
    zero = jnp.zeros_like(qg)
    return jnp.where(low, qg, zero), jnp.where(low, zero, qg)


def local_part(at_ref, kv_ref, q0, q1, q2, q3, out_ref, s_ref, gp_ref, terms_ref):
    x = at_ref[0]
    q, g = halves(jnp.concatenate([q0[...], q1[...], q2[...], q3[...]], axis=0))
    kv = kv_ref[...]
    for r in range(0, ROWS, 128):
        rows = slice(r, r + 128)
        s_ref[rows, :] = dot(q[rows], kv, NT)
        gp_ref[rows, :] = dot(g[rows], kv, NT)
    blocks = [slice(j, j + 128) for j in range(0, MEMS, 128)]
    lses, means = [], []
    for r in range(0, ROWS, 128):
        rows = slice(r, r + 128)
        top = s_ref[rows, blocks[0]]
        for j in blocks[1:]:
            top = jnp.maximum(top, s_ref[rows, j])
        peak = jnp.max(top, axis=1, keepdims=True)
        total = jnp.zeros((128, 128), F32)
        weighted = jnp.zeros((128, 128), F32)
        for j in blocks:
            e = jnp.exp(s_ref[rows, j] - peak)
            s_ref[rows, j] = e
            total += e
            weighted += e * gp_ref[rows, j]
        total = jnp.sum(total, axis=1, keepdims=True)
        inverse = 1.0 / total
        mean = jnp.sum(weighted, axis=1, keepdims=True) * inverse
        lses.append(peak + jnp.log(total))
        means.append(mean)
        for j in blocks:
            prob = s_ref[rows, j] * inverse
            terms_ref[rows, j] = (prob * (gp_ref[rows, j] - mean)).astype(BF16)
            terms_ref[ROWS + r : ROWS + r + 128, j] = prob.astype(BF16)
    both = dot(terms_ref[...], kv, NN)
    both = jnp.where(low_lanes((ROWS, 128)), both[:ROWS], pltpu.roll(both[ROWS:], 64, 1))
    first = lax.broadcasted_iota(jnp.int32, (128, 128), 1) == 0
    turned = [jnp.where(first, a, b).T for a, b in zip(lses, means)]
    lse = jnp.concatenate([a[0:1] for a in turned], axis=1)
    mean = jnp.concatenate([a[1:2] for a in turned], axis=1)
    pad = jnp.zeros((1, 128 - MINE), F32)
    for r in range(NX):
        owner = lax.rem(x - r + NX, NX)
        own = [jnp.concatenate([a[:, MINE * r : MINE * r + MINE], pad], axis=1) for a in (lse, mean)]
        for z in range(NZ):
            t = 128 * min(z, 2)
            a = MINE * r + 8 * z
            b = MINE * r + 64 + 4 * z
            out_ref[owner * NZ + z, 0:8, :] = both[a : a + 8, :]
            rows = [both[b : b + 4, :], lse[:, t : t + 128], mean[:, t : t + 128]] + own
            out_ref[owner * NZ + z, 8:16, :] = jnp.concatenate(rows, axis=0)


def weights(logs, means):
    peak = jnp.max(logs, axis=0, keepdims=True)
    e = jnp.exp(logs - peak)
    total = jnp.sum(e, axis=0, keepdims=True)
    w = e / total
    offset = jnp.sum(w * means, axis=0, keepdims=True)
    return peak + jnp.log(total), offset, w


def three(a):
    first = a.astype(BF16).astype(F32)
    second = (a - first).astype(BF16).astype(F32)
    return [first, second, a - first - second]


def add_query(at_ref, in_ref, out_ref, col_ref):
    z, x = at_ref[0], at_ref[1]
    odd = lax.rem(z, 2) == 1
    low = low_lanes((8, 128))
    top = lax.broadcasted_iota(jnp.int32, (8, 128), 0) < 4
    full, half = [], []
    for u in range(NX):
        logs = jnp.concatenate([in_ref[u * NZ + d, 14:15, :] for d in range(NZ)], axis=0)
        means = jnp.concatenate([in_ref[u * NZ + d, 15:16, :] for d in range(NZ)], axis=0)
        _, offset, w = weights(logs, means)
        shift = w * (means - offset)
        col_ref[u] = jnp.concatenate([w, shift, jnp.zeros((112, 128), F32)], axis=0).T
        cols = col_ref[u, pl.ds(pl.multiple_of(8 * z, 8), 8), :]
        ends = col_ref[u, pl.ds(pl.multiple_of(64 + 8 * (z // 2), 8), 8), :]
        ends = jnp.where(odd, pltpu.roll(ends, 4, 0), ends)
        a = jnp.zeros((8, 128), F32)
        b = jnp.zeros((8, 128), F32)
        for d in range(NZ):
            tile = in_ref[u * NZ + d]
            a += tile[0:8] * jnp.where(low, cols[:, d : d + 1], cols[:, 8 + d : 9 + d])
            b += tile[8:16] * jnp.where(low, ends[:, d : d + 1], ends[:, 8 + d : 9 + d])
        full.append(a + pltpu.roll(a, 64, 1))
        half.append(b + pltpu.roll(b, 64, 1))
    f = [jnp.where(low, full[2 * p], full[2 * p + 1]) for p in range(2)]
    h = [jnp.where(low, half[2 * p], half[2 * p + 1]) for p in range(2)]
    logs = jnp.concatenate([in_ref[x * NZ + d, 12:13, :] for d in range(NZ)], axis=0)
    means = jnp.concatenate([in_ref[x * NZ + d, 13:14, :] for d in range(NZ)], axis=0)
    lse, offset, _ = weights(logs, means)
    stats = three(lse) + three(offset) + [jnp.zeros((2, 128), F32)]
    piece = jnp.concatenate([f[0], f[1], jnp.where(top, h[0], pltpu.roll(h[1], 4, 0))] + stats, axis=0)
    out_ref[...] = jnp.broadcast_to(piece.astype(BF16)[None], out_ref.shape)


def by_core(at_ref, a, b):
    first = at_ref[0] == 0
    return jnp.where(first, a, b), jnp.where(first, b, a)


def join_rows(at_ref, own_ref, other_ref, out_ref, y, z4):
    low = low_lanes((8, 128))
    top = lax.broadcasted_iota(jnp.int32, (8, 128), 0) < 4

    def heads(f0, f1):
        return jnp.where(low, f0, pltpu.roll(f1, 64, 1)), jnp.where(low, pltpu.roll(f0, 64, 1), f1)

    where = [y * NZ + z4 + i for i in range(4)]
    pairs = [by_core(at_ref, own_ref[w].astype(F32), other_ref[w].astype(F32)) for w in where]
    pieces = [[pairs[i][c] for i in range(4)] for c in range(NC)]
    for p in range(2):
        tiles = [heads(pieces[0][i][8 * p : 8 * p + 8], pieces[1][i][8 * p : 8 * p + 8]) for i in range(4)]
        ends = []
        for i in (0, 2):
            g = []
            for c in range(NC):
                even, odd = pieces[c][i][16:24], pieces[c][i + 1][16:24]
                if p == 0:
                    g.append(jnp.where(top, even, pltpu.roll(odd, 4, 0)))
                else:
                    g.append(jnp.where(top, pltpu.roll(even, 4, 0), odd))
            ends.append(heads(g[0], g[1]))
        for u in range(2):
            lanes = slice(((2 * p + u) * NY + y) * 128, ((2 * p + u) * NY + y) * 128 + 128)
            for i in (0, 2):
                r = 8 * (z4 + i)
                both = jnp.concatenate([tiles[i][u], tiles[i + 1][u]], axis=0)
                out_ref[r : r + 16, lanes] = both.astype(BF16)
            r = 64 + 4 * z4
            both = jnp.concatenate([ends[0][u], ends[1][u]], axis=0)
            out_ref[r : r + 16, lanes] = both.astype(BF16)


def sender(sems):
    copies = []

    def send(src, dst):
        copy = pltpu.make_async_copy(src, dst, sems.at[len(copies)])
        copy.start()
        copies.append(copy)

    return copies, send


def join_query(at_ref, own_ref, other_ref, q_hbm, q_ref, sems):
    copies, send = sender(sems)
    for z4 in range(0, NZ, 4):
        for y in range(NY):
            join_rows(at_ref, own_ref, other_ref, q_ref, y, z4)
        for start, size in ((8 * z4, 32), (64 + 4 * z4, 16)):
            rows = pl.ds(start, size)
            send(q_ref.at[rows, :], q_hbm.at[rows, :])
    for copy in copies:
        copy.wait()


def join_memory(at_ref, grads_ref, sent_ref, k_hbm, v_hbm, k_ref, v_ref, sems):
    copies, send = sender(sems)
    low = low_lanes((BLOCK, 128))
    for y in range(NY):
        a, b = by_core(at_ref, grads_ref[y].astype(F32), sent_ref[y].astype(F32))
        lanes = slice(128 * y, 128 * y + 128)
        k_ref[:, lanes] = jnp.where(low, a, pltpu.roll(b, 64, 1)).astype(BF16)
        v_ref[:, lanes] = jnp.where(low, pltpu.roll(a, 64, 1), b).astype(BF16)
        if y % 2 == 1:
            part = pl.ds(128 * (y - 1), 256)
            send(k_ref.at[:, part], k_hbm.at[:, part])
            send(v_ref.at[:, part], v_hbm.at[:, part])
    for copy in copies:
        copy.wait()


def head_grads(told_ref, y, kv, qs):
    logs, offsets = [], []
    for t in range(3):
        piece = told_ref[y * NZ + t].astype(F32)
        logs.append(piece[24:25] + piece[25:26] + piece[26:27])
        offsets.append(piece[27:28] + piece[28:29] + piece[29:30])
    lse = jnp.concatenate(logs, axis=1)
    offset = jnp.concatenate(offsets, axis=1)
    q, g = halves(jnp.concatenate([q_ref[y] for q_ref in qs], axis=0))
    prob = jnp.exp(dot(kv, q, NT) - lse)
    ds = (prob * (dot(kv, g, NT) - offset)).astype(BF16)
    return dot(ds, q, NN) + dot(prob.astype(BF16), g, NN)


def chip_grads(told_ref, own_ref, away_ref, q0, q1, q2, q3, mine_ref, sent_ref):
    for y in range(NY):
        kv = jnp.concatenate([own_ref[y], away_ref[y]], axis=0)
        out = head_grads(told_ref, y, kv, (q0, q1, q2, q3)).astype(BF16)
        mine_ref[y] = out[:BLOCK]
        sent_ref[y] = out[BLOCK:]


def around(parts):
    return parts[:1] + [
        lax.ppermute(parts[k], "row", [(i, (i + k) % NX) for i in range(NX)]) for k in range(1, NX)
    ]


def local(query, out_grad, keys, values):
    shape = jax.ShapeDtypeStruct
    z, y, c = lax.axis_index("z"), lax.axis_index("y"), lax.axis_index("core")
    x = lax.axis_index("row")
    at = jnp.stack([x, y, c]).astype(jnp.int32)
    zx = jnp.stack([z, x]).astype(jnp.int32)
    corez = c.astype(jnp.int32)[None]
    mega = 2**20

    half = shape((NY, BLOCK, 128), BF16)
    home = pl.pallas_call(
        pack_memory,
        out_shape=shape((HEADS, BLOCK, 128), BF16),
        in_specs=[pl.BlockSpec(memory_space=pl.ANY)] * 2,
        out_specs=VMEM,
        scratch_shapes=[pltpu.VMEM((BLOCK, 1024), BF16)] * 2 + [pltpu.SemaphoreType.DMA((2, 2))],
        compiler_params=pltpu.CompilerParams(vmem_limit_bytes=60 * 2**20),
        cost_estimate=pl.CostEstimate(flops=0, bytes_accessed=mega, transcendentals=0),
    )(keys, values)
    memory = lax.all_to_all(home, ("core", "y"), 0, 0, tiled=True).reshape(MEMS, 128)
    mine = call(pack_mine, [shape((MINE, 128), BF16)] * NX, 2, smem=1, moved=mega)(at, query, out_grad)
    mine = around(list(mine))
    home_own, home_away = call(split_heads, [half, half], 1, smem=1, moved=mega)(corez, home)
    away = lax.ppermute(home_away, "core", SWAP)

    work = 2 * MEMS * ROWS * 128
    part = call(
        local_part,
        shape((NZ * NX, 16, 128), F32),
        5,
        smem=1,
        scratch=[pltpu.VMEM((ROWS, MEMS), F32)] * 2 + [pltpu.VMEM((2 * ROWS, MEMS), BF16)],
        flops=4 * work,
        moved=mega,
        exps=MEMS * ROWS,
    )(at, memory, *mine)
    part = lax.all_to_all(part, ("row", "z"), 0, 0, tiled=True)
    heads = call(pack_query, [shape((NY, MINE, 128), BF16)] * NX, 2, smem=1, moved=3 * mega)(at, query, out_grad)
    part, away, *heads = lax.optimization_barrier((part, away, *heads))
    piece = call(
        add_query,
        shape((NZ * NY, 32, 128), BF16),
        1,
        smem=1,
        scratch=[pltpu.VMEM((NX, 128, 128), F32)],
        moved=mega,
    )(zx, part)
    piece = lax.all_to_all(piece, ("y", "z"), 0, 0, tiled=True)
    heads = around(list(heads))
    piece, *heads = lax.optimization_barrier((piece, *heads))
    other = lax.ppermute(piece, "core", SWAP)
    grads, sent = call(chip_grads, [half, half], 7, flops=4 * work, moved=2 * mega, exps=MEMS * ROWS)(
        piece, home_own, away, *heads
    )
    sent = lax.ppermute(sent, "core", SWAP)
    def joined(body, results, count):
        return pl.pallas_call(
            body,
            out_shape=results,
            in_specs=[SMEM] + [VMEM] * 2,
            out_specs=[pl.BlockSpec(memory_space=pl.ANY)] * len(results),
            scratch_shapes=[pltpu.VMEM(a.shape, a.dtype) for a in results] + [pltpu.SemaphoreType.DMA((count,))],
            compiler_params=pltpu.CompilerParams(vmem_limit_bytes=24 * 2**20),
            cost_estimate=pl.CostEstimate(flops=0, bytes_accessed=2 * mega, transcendentals=0),
        )

    (query_grad,) = joined(join_query, [shape((MINE, 4096), BF16)], 4)(corez, piece, other)
    sent, query_grad = lax.optimization_barrier((sent, query_grad))
    key_grad, value_grad = joined(join_memory, [shape((BLOCK, 1024), BF16)] * 2, 8)(corez, grads, sent)
    return (query_grad, key_grad, value_grad)


def solution(mesh):
    fine = Mesh(mesh.devices.reshape(NZ, NY, NC, NX), ("z", "y", "core", "row"))
    psg = ("z", "y", "core")
    placed = (P("row", None), P("row", None), P(psg, "row"), P(psg, "row"))
    return jax.shard_map(
        local,
        mesh=fine,
        in_specs=placed,
        out_specs=(P("row", None), P(psg, "row"), P(psg, "row")),
        check_vma=False,
    )
```

```python
import jax
import jax.numpy as jnp
from jax import lax
from jax.experimental import pallas as pl
from jax.experimental.pallas import tpu as pltpu
from jax.sharding import Mesh
from jax.sharding import PartitionSpec as P

F32 = jnp.float32
BF16 = jnp.bfloat16
NZ, NY, NC, NX = 8, 8, 2, 4
HEADS = 16
BLOCK = 128
ROWS = 384
MINE = ROWS // NX
MEMS = HEADS * BLOCK
STEP = 256
NT = (((1,), (1,)), ((), ()))
TN = (((0,), (0,)), ((), ()))
SWAP = [(0, 1), (1, 0)]
NN = (((1,), (0,)), ((), ()))

VMEM = pl.BlockSpec(memory_space=pltpu.VMEM)
SMEM = pl.BlockSpec(memory_space=pltpu.SMEM)


def call(body, out_shape, n_in, scratch=(), smem=0, flops=0, moved=0, exps=0):
    outs = out_shape if isinstance(out_shape, (tuple, list)) else None
    return pl.pallas_call(
        body,
        out_shape=out_shape,
        in_specs=[SMEM] * smem + [VMEM] * n_in,
        out_specs=[VMEM] * len(outs) if outs else VMEM,
        scratch_shapes=list(scratch),
        compiler_params=pltpu.CompilerParams(vmem_limit_bytes=24 * 2**20),
        cost_estimate=pl.CostEstimate(flops=flops, bytes_accessed=moved, transcendentals=exps),
    )


def dot(a, b, dims):
    return lax.dot_general(a, b, dims, preferred_element_type=F32)


def low_lanes(shape):
    return lax.broadcasted_iota(jnp.int32, shape, len(shape) - 1) < 64


def pack_memory(k_hbm, v_hbm, out_ref, k_ref, v_ref, sems):
    copies = []
    for i in range(2):
        lanes = pl.ds(512 * i, 512)
        copies.append(pltpu.make_async_copy(k_hbm.at[:, lanes], k_ref.at[:, lanes], sems.at[0, i]))
        copies.append(pltpu.make_async_copy(v_hbm.at[:, lanes], v_ref.at[:, lanes], sems.at[1, i]))
    for copy in copies:
        copy.start()
    for t in range(HEADS // 2):
        if t % 4 == 0:
            copies[t // 2].wait()
            copies[t // 2 + 1].wait()
        k = k_ref[:, 128 * t : 128 * t + 128]
        v = v_ref[:, 128 * t : 128 * t + 128]
        out_ref[2 * t] = jnp.concatenate([k[:, :64], v[:, :64]], axis=1)
        out_ref[2 * t + 1] = jnp.concatenate([k[:, 64:], v[:, 64:]], axis=1)


def split_heads(core_ref, in_ref, own_ref, away_ref):
    c = core_ref[0]
    for t in range(HEADS // 2):
        own_ref[t] = in_ref[2 * t + c]
        away_ref[t] = in_ref[2 * t + 1 - c]


def pack_mine(at_ref, q_ref, g_ref, *outs):
    x, y, c = at_ref[0], at_ref[1], at_ref[2]
    low = low_lanes((MINE, 128))
    for k in range(NX):
        lanes = pl.ds(pl.multiple_of((lax.rem(x + k, NX) * NY + y) * 128, 128), 128)
        q = q_ref[:, lanes].astype(F32)
        g = g_ref[:, lanes].astype(F32)
        first = jnp.where(low, q, pltpu.roll(g, 64, 1))
        second = jnp.where(low, pltpu.roll(q, 64, 1), g)
        outs[k][...] = jnp.where(c == 0, first, second).astype(BF16)


def pack_query(at_ref, q_ref, g_ref, *outs):
    x, c = at_ref[0], at_ref[2]
    low = low_lanes((MINE, 128))
    for k in range(NX):
        start = lax.rem(x + k, NX) * 1024
        for t in range(HEADS // 2):
            lanes = pl.ds(pl.multiple_of(start + 128 * t, 128), 128)
            q = q_ref[:, lanes].astype(F32)
            g = g_ref[:, lanes].astype(F32)
            first = jnp.where(low, q, pltpu.roll(g, 64, 1))
            second = jnp.where(low, pltpu.roll(q, 64, 1), g)
            outs[k][t] = jnp.where(c == 0, first, second).astype(BF16)


def halves(qg):
    low = low_lanes(qg.shape)
    zero = jnp.zeros_like(qg)
    return jnp.where(low, qg, zero), jnp.where(low, zero, qg)


def local_part(at_ref, kv_ref, q0, q1, q2, q3, out_ref, s_ref, gp_ref, terms_ref):
    x = at_ref[0]
    q, g = halves(jnp.concatenate([q0[...], q1[...], q2[...], q3[...]], axis=0))
    kv = kv_ref[...]
    for r in range(0, ROWS, 128):
        rows = slice(r, r + 128)
        s_ref[rows, :] = dot(q[rows], kv, NT)
        gp_ref[rows, :] = dot(g[rows], kv, NT)
    blocks = [slice(j, j + 128) for j in range(0, MEMS, 128)]
    lses, means = [], []
    for r in range(0, ROWS, 128):
        rows = slice(r, r + 128)
        top = s_ref[rows, blocks[0]]
        for j in blocks[1:]:
            top = jnp.maximum(top, s_ref[rows, j])
        peak = jnp.max(top, axis=1, keepdims=True)
        total = jnp.zeros((128, 128), F32)
        weighted = jnp.zeros((128, 128), F32)
        for j in blocks:
            e = jnp.exp(s_ref[rows, j] - peak)
            s_ref[rows, j] = e
            total += e
            weighted += e * gp_ref[rows, j]
        total = jnp.sum(total, axis=1, keepdims=True)
        inverse = 1.0 / total
        mean = jnp.sum(weighted, axis=1, keepdims=True) * inverse
        lses.append(peak + jnp.log(total))
        means.append(mean)
        for j in blocks:
            prob = s_ref[rows, j] * inverse
            terms_ref[rows, j] = (prob * (gp_ref[rows, j] - mean)).astype(BF16)
            terms_ref[ROWS + r : ROWS + r + 128, j] = prob.astype(BF16)
    both = dot(terms_ref[...], kv, NN)
    both = jnp.where(low_lanes((ROWS, 128)), both[:ROWS], pltpu.roll(both[ROWS:], 64, 1))
    first = lax.broadcasted_iota(jnp.int32, (128, 128), 1) == 0
    turned = [jnp.where(first, a, b).T for a, b in zip(lses, means)]
    lse = jnp.concatenate([a[0:1] for a in turned], axis=1)
    mean = jnp.concatenate([a[1:2] for a in turned], axis=1)
    pad = jnp.zeros((1, 128 - MINE), F32)
    for r in range(NX):
        owner = lax.rem(x - r + NX, NX)
        own = [jnp.concatenate([a[:, MINE * r : MINE * r + MINE], pad], axis=1) for a in (lse, mean)]
        for z in range(NZ):
            t = 128 * min(z, 2)
            a = MINE * r + 8 * z
            b = MINE * r + 64 + 4 * z
            out_ref[owner * NZ + z, 0:8, :] = both[a : a + 8, :]
            rows = [both[b : b + 4, :], lse[:, t : t + 128], mean[:, t : t + 128]] + own
            out_ref[owner * NZ + z, 8:16, :] = jnp.concatenate(rows, axis=0)


def weights(logs, means):
    peak = jnp.max(logs, axis=0, keepdims=True)
    e = jnp.exp(logs - peak)
    total = jnp.sum(e, axis=0, keepdims=True)
    w = e / total
    offset = jnp.sum(w * means, axis=0, keepdims=True)
    return peak + jnp.log(total), offset, w


def three(a):
    first = a.astype(BF16).astype(F32)
    second = (a - first).astype(BF16).astype(F32)
    return [first, second, a - first - second]


def add_query(at_ref, in_ref, out_ref, col_ref):
    z, x = at_ref[0], at_ref[1]
    odd = lax.rem(z, 2) == 1
    low = low_lanes((8, 128))
    top = lax.broadcasted_iota(jnp.int32, (8, 128), 0) < 4
    full, half = [], []
    for u in range(NX):
        logs = jnp.concatenate([in_ref[u * NZ + d, 14:15, :] for d in range(NZ)], axis=0)
        means = jnp.concatenate([in_ref[u * NZ + d, 15:16, :] for d in range(NZ)], axis=0)
        _, offset, w = weights(logs, means)
        shift = w * (means - offset)
        col_ref[u] = jnp.concatenate([w, shift, jnp.zeros((112, 128), F32)], axis=0).T
        cols = col_ref[u, pl.ds(pl.multiple_of(8 * z, 8), 8), :]
        ends = col_ref[u, pl.ds(pl.multiple_of(64 + 8 * (z // 2), 8), 8), :]
        ends = jnp.where(odd, pltpu.roll(ends, 4, 0), ends)
        a = jnp.zeros((8, 128), F32)
        b = jnp.zeros((8, 128), F32)
        for d in range(NZ):
            tile = in_ref[u * NZ + d]
            a += tile[0:8] * jnp.where(low, cols[:, d : d + 1], cols[:, 8 + d : 9 + d])
            b += tile[8:16] * jnp.where(low, ends[:, d : d + 1], ends[:, 8 + d : 9 + d])
        full.append(a + pltpu.roll(a, 64, 1))
        half.append(b + pltpu.roll(b, 64, 1))
    f = [jnp.where(low, full[2 * p], full[2 * p + 1]) for p in range(2)]
    h = [jnp.where(low, half[2 * p], half[2 * p + 1]) for p in range(2)]
    logs = jnp.concatenate([in_ref[x * NZ + d, 12:13, :] for d in range(NZ)], axis=0)
    means = jnp.concatenate([in_ref[x * NZ + d, 13:14, :] for d in range(NZ)], axis=0)
    lse, offset, _ = weights(logs, means)
    stats = three(lse) + three(offset) + [jnp.zeros((2, 128), F32)]
    piece = jnp.concatenate([f[0], f[1], jnp.where(top, h[0], pltpu.roll(h[1], 4, 0))] + stats, axis=0)
    out_ref[...] = jnp.broadcast_to(piece.astype(BF16)[None], out_ref.shape)


def by_core(at_ref, a, b):
    first = at_ref[0] == 0
    return jnp.where(first, a, b), jnp.where(first, b, a)


def join_rows(at_ref, own_ref, other_ref, out_ref, y, z4):
    low = low_lanes((8, 128))
    top = lax.broadcasted_iota(jnp.int32, (8, 128), 0) < 4

    def heads(f0, f1):
        return jnp.where(low, f0, pltpu.roll(f1, 64, 1)), jnp.where(low, pltpu.roll(f0, 64, 1), f1)

    where = [y * NZ + z4 + i for i in range(4)]
    pairs = [by_core(at_ref, own_ref[w].astype(F32), other_ref[w].astype(F32)) for w in where]
    pieces = [[pairs[i][c] for i in range(4)] for c in range(NC)]
    for p in range(2):
        tiles = [heads(pieces[0][i][8 * p : 8 * p + 8], pieces[1][i][8 * p : 8 * p + 8]) for i in range(4)]
        ends = []
        for i in (0, 2):
            g = []
            for c in range(NC):
                even, odd = pieces[c][i][16:24], pieces[c][i + 1][16:24]
                if p == 0:
                    g.append(jnp.where(top, even, pltpu.roll(odd, 4, 0)))
                else:
                    g.append(jnp.where(top, pltpu.roll(even, 4, 0), odd))
            ends.append(heads(g[0], g[1]))
        for u in range(2):
            lanes = slice(((2 * p + u) * NY + y) * 128, ((2 * p + u) * NY + y) * 128 + 128)
            for i in (0, 2):
                r = 8 * (z4 + i)
                both = jnp.concatenate([tiles[i][u], tiles[i + 1][u]], axis=0)
                out_ref[r : r + 16, lanes] = both.astype(BF16)
            r = 64 + 4 * z4
            both = jnp.concatenate([ends[0][u], ends[1][u]], axis=0)
            out_ref[r : r + 16, lanes] = both.astype(BF16)


def sender(sems):
    copies = []

    def send(src, dst):
        copy = pltpu.make_async_copy(src, dst, sems.at[len(copies)])
        copy.start()
        copies.append(copy)

    return copies, send


def join_query(at_ref, own_ref, other_ref, q_hbm, q_ref, sems):
    copies, send = sender(sems)
    for z4 in range(0, NZ, 4):
        for y in range(NY):
            join_rows(at_ref, own_ref, other_ref, q_ref, y, z4)
        for start, size in ((8 * z4, 32), (64 + 4 * z4, 16)):
            rows = pl.ds(start, size)
            send(q_ref.at[rows, :], q_hbm.at[rows, :])
    for copy in copies:
        copy.wait()


def join_memory(at_ref, grads_ref, sent_ref, k_hbm, v_hbm, k_ref, v_ref, sems):
    copies, send = sender(sems)
    for y in range(NY):
        a, b = by_core(at_ref, grads_ref[y], sent_ref[y])
        lanes = slice(128 * y, 128 * y + 128)
        k_ref[:, lanes] = jnp.concatenate([a[:, :64], b[:, :64]], axis=1)
        v_ref[:, lanes] = jnp.concatenate([a[:, 64:], b[:, 64:]], axis=1)
        if y % 2 == 1:
            part = pl.ds(128 * (y - 1), 256)
            send(k_ref.at[:, part], k_hbm.at[:, part])
            send(v_ref.at[:, part], v_hbm.at[:, part])
    for copy in copies:
        copy.wait()


def head_grads(told_ref, y, kv, qs):
    logs, offsets = [], []
    for t in range(3):
        piece = told_ref[y * NZ + t].astype(F32)
        logs.append(piece[24:25] + piece[25:26] + piece[26:27])
        offsets.append(piece[27:28] + piece[28:29] + piece[29:30])
    lse = jnp.concatenate(logs, axis=1)
    offset = jnp.concatenate(offsets, axis=1)
    q, g = halves(jnp.concatenate([q_ref[y] for q_ref in qs], axis=0))
    prob = jnp.exp(dot(kv, q, NT) - lse)
    ds = (prob * (dot(kv, g, NT) - offset)).astype(BF16)
    return dot(ds, q, NN) + dot(prob.astype(BF16), g, NN)


def chip_grads(told_ref, own_ref, away_ref, q0, q1, q2, q3, mine_ref, sent_ref):
    for y in range(NY):
        kv = jnp.concatenate([own_ref[y], away_ref[y]], axis=0)
        out = head_grads(told_ref, y, kv, (q0, q1, q2, q3)).astype(BF16)
        mine_ref[y] = out[:BLOCK]
        sent_ref[y] = out[BLOCK:]


def around(parts):
    return parts[:1] + [
        lax.ppermute(parts[k], "row", [(i, (i + k) % NX) for i in range(NX)]) for k in range(1, NX)
    ]


def local(query, out_grad, keys, values):
    shape = jax.ShapeDtypeStruct
    z, y, c = lax.axis_index("z"), lax.axis_index("y"), lax.axis_index("core")
    x = lax.axis_index("row")
    at = jnp.stack([x, y, c]).astype(jnp.int32)
    zx = jnp.stack([z, x]).astype(jnp.int32)
    corez = c.astype(jnp.int32)[None]
    mega = 2**20

    half = shape((NY, BLOCK, 128), BF16)
    home = pl.pallas_call(
        pack_memory,
        out_shape=shape((HEADS, BLOCK, 128), BF16),
        in_specs=[pl.BlockSpec(memory_space=pl.ANY)] * 2,
        out_specs=VMEM,
        scratch_shapes=[pltpu.VMEM((BLOCK, 1024), BF16)] * 2 + [pltpu.SemaphoreType.DMA((2, 2))],
        compiler_params=pltpu.CompilerParams(vmem_limit_bytes=60 * 2**20),
        cost_estimate=pl.CostEstimate(flops=0, bytes_accessed=mega, transcendentals=0),
    )(keys, values)
    memory = lax.all_to_all(home, ("y", "core"), 0, 0, tiled=True).reshape(MEMS, 128)
    mine = call(pack_mine, [shape((MINE, 128), BF16)] * NX, 2, smem=1, moved=mega)(at, query, out_grad)
    mine = around(list(mine))
    home_own, home_away = call(split_heads, [half, half], 1, smem=1, moved=mega)(corez, home)
    away = lax.ppermute(home_away, "core", SWAP)

    work = 2 * MEMS * ROWS * 128
    part = call(
        local_part,
        shape((NZ * NX, 16, 128), F32),
        5,
        smem=1,
        scratch=[pltpu.VMEM((ROWS, MEMS), F32)] * 2 + [pltpu.VMEM((2 * ROWS, MEMS), BF16)],
        flops=4 * work,
        moved=mega,
        exps=MEMS * ROWS,
    )(at, memory, *mine)
    part = lax.all_to_all(part, ("row", "z"), 0, 0, tiled=True)
    heads = call(pack_query, [shape((NY, MINE, 128), BF16)] * NX, 2, smem=1, moved=3 * mega)(at, query, out_grad)
    part, away, *heads = lax.optimization_barrier((part, away, *heads))
    piece = call(
        add_query,
        shape((NZ * NY, 32, 128), BF16),
        1,
        smem=1,
        scratch=[pltpu.VMEM((NX, 128, 128), F32)],
        moved=mega,
    )(zx, part)
    piece = lax.all_to_all(piece, ("y", "z"), 0, 0, tiled=True)
    heads = around(list(heads))
    piece, *heads = lax.optimization_barrier((piece, *heads))
    other = lax.ppermute(piece, "core", SWAP)
    grads, sent = call(chip_grads, [half, half], 7, flops=4 * work, moved=2 * mega, exps=MEMS * ROWS)(
        piece, home_own, away, *heads
    )
    sent = lax.ppermute(sent, "core", SWAP)
    def joined(body, results, count):
        return pl.pallas_call(
            body,
            out_shape=results,
            in_specs=[SMEM] + [VMEM] * 2,
            out_specs=[pl.BlockSpec(memory_space=pl.ANY)] * len(results),
            scratch_shapes=[pltpu.VMEM(a.shape, a.dtype) for a in results] + [pltpu.SemaphoreType.DMA((count,))],
            compiler_params=pltpu.CompilerParams(vmem_limit_bytes=24 * 2**20),
            cost_estimate=pl.CostEstimate(flops=0, bytes_accessed=2 * mega, transcendentals=0),
        )

    (query_grad,) = joined(join_query, [shape((MINE, 4096), BF16)], 4)(corez, piece, other)
    sent, query_grad = lax.optimization_barrier((sent, query_grad))
    key_grad, value_grad = joined(join_memory, [shape((BLOCK, 1024), BF16)] * 2, 8)(corez, grads, sent)
    return (query_grad, key_grad, value_grad)


def solution(mesh):
    fine = Mesh(mesh.devices.reshape(NZ, NY, NC, NX), ("z", "y", "core", "row"))
    psg = ("z", "y", "core")
    placed = (P("row", None), P("row", None), P(psg, "row"), P(psg, "row"))
    return jax.shard_map(
        local,
        mesh=fine,
        in_specs=placed,
        out_specs=(P("row", None), P(psg, "row"), P(psg, "row")),
        check_vma=False,
    )
```
